256 devices in a mesh: section: 16 (over x_lo, z), row: 2 (over x_hi), col: 8 (over y, core).
Axes of the slice: x: 4 (x_hi: 2, x_lo: 2; x = x_hi * 2 + x_lo), y: 4, z: 8, core: 2. Of those that a mesh axis runs over, the one named last changes fastest.
Arguments:
- input_fwd: bfloat16 [16, 256, 2560], P('section', 'col', 'row'), may hold values from -6 to 6
- input_bwd: bfloat16 [16, 256, 2560], P('section', 'col', 'row'), may hold values from -6 to 6
- cotangent: bfloat16 [16, 256, 2560], P('section', 'col', 'row'), may hold values from -0.375 to 0.375
- shared_up: bfloat16 [2560, 16384], P('row', ('col', 'section')), may hold values from -0.125 to 0.125
- shared_down: bfloat16 [16384, 2560], P(('col', 'section'), 'row'), may hold values from -0.046875 to 0.046875
- up_left: bfloat16 [16, 2560, 256], P('section', 'row'), may hold values from -0.125 to 0.125
- up_right: bfloat16 [16, 256, 16384], P('section', None, 'col'), may hold values from -0.1875 to 0.1875
- down_left: bfloat16 [16, 16384, 256], P('section', 'col'), may hold values from -0.046875 to 0.046875
- down_right: bfloat16 [16, 256, 2560], P('section', None, 'row'), may hold values from -0.1875 to 0.1875
Outputs:
- handoff_fwd: bfloat16 [16, 256, 2560], P('section', 'col', 'row')
- handoff_bwd: bfloat16 [16, 256, 2560], P('section', 'col', 'row')
- grad_shared_up: bfloat16 [2560, 16384], P('row', ('col', 'section'))
- grad_shared_down: bfloat16 [16384, 2560], P(('col', 'section'), 'row')
- grad_up_left: float32 [16, 2560, 256], P('section', 'row')
- grad_up_right: float32 [16, 256, 16384], P('section', None, 'col')
- grad_down_left: float32 [16, 16384, 256], P('section', 'col')
- grad_down_right: float32 [16, 256, 2560], P('section', None, 'row')
The draws below stay inside these ranges and needn't reach their ends.
All inputs are finite; a program needn't handle non-finite values.
Results may differ from the reference program's by a relative error of at most 0.022.
Values may be sent and summed in bfloat16 or wider, within the bound.
No kernel may reach another device: no remote copies, remote signals or barrier semaphores. Data moves between devices by JAX's collectives and lax.ppermute only.
A program may use at most 128 MiB of HBM per device.

```python
import jax
import jax.numpy as jnp
from jax import lax

D = 2560
FF = 16384
R = 256
MICRO = 256
SECTIONS = 16


def shard_levels(stream_key, shape, shards, low, largest):
    factor_of, own = 1.0, jax.random.fold_in(stream_key, 6)
    for dim, blocks in shards:
        draws = jnp.exp(jax.random.uniform(jax.random.fold_in(own, dim), (blocks,), jnp.float32, low / len(shards), largest / len(shards)))
        factor_of = factor_of * jnp.repeat(draws, shape[dim] // blocks).reshape([-1 if axis == dim else 1 for axis in range(len(shape))])
    return factor_of


def centred(key, extent, scale, bound, cuts=(), dtype=jnp.bfloat16):
    drawn = jax.random.normal(key, extent, jnp.float32) * scale
    if len(cuts) > 0:
        drawn = shard_levels(key, extent, cuts, -0.22, 0.18) * drawn
    return jnp.clip(drawn, min=-bound, max=bound).astype(dtype)


def setup_inputs(seed: int = 0) -> dict:
    keys = jax.random.split(jax.random.key(seed), 10)
    return {
        "input_fwd": centred(keys[0], (SECTIONS, MICRO, D), 1.0, 6.0, ((0, 16), (1, 8), (2, 2))),
        "input_bwd": centred(keys[1], (SECTIONS, MICRO, D), 1.0, 6.0, ((0, 16), (1, 8), (2, 2))),
        "cotangent": centred(keys[2], (SECTIONS, MICRO, D), (MICRO ** -0.5), 0.375, ((0, 16), (1, 8), (2, 2))),
        "shared_up": centred(keys[3], (D, FF), D ** -0.5, 0.125, ((0, 2), (1, 128))),
        "shared_down": centred(keys[4], (FF, D), FF ** -0.5, 0.046875, ((0, 128), (1, 2))),
        "up_left": centred(keys[5], (SECTIONS, D, R), D ** -0.5, 0.125, ((0, 16), (1, 2))),
        "up_right": centred(keys[6], (SECTIONS, R, FF), (0.5 * R ** -0.5), 0.1875, ((0, 16), (2, 8))),
        "down_left": centred(keys[7], (SECTIONS, FF, R), FF ** -0.5, 0.046875, ((0, 16), (1, 8))),
        "down_right": centred(keys[8], (SECTIONS, R, D), (0.5 * R ** -0.5), 0.1875, ((0, 16), (2, 2))),
    }


def product(left, right):
    return jnp.dot(left, right, preferred_element_type=jnp.float32)


def silu_slope(preact):
    sigma = jax.nn.sigmoid(preact)
    return sigma * (1.0 + preact * (1.0 - sigma))


def one_section(shared_up, shared_down, section_data):
    input_fwd, input_bwd, cotangent, up_left, up_right, down_left, down_right = section_data
    count_fwd = input_fwd.shape[0]
    normed = jnp.concatenate([input_fwd, input_bwd], axis=0)
    delta_in = product(normed, up_left).astype(jnp.bfloat16)
    preact = product(normed, shared_up) + product(delta_in, up_right)
    hidden = jax.nn.silu(preact).astype(jnp.bfloat16)
    delta_out = product(hidden, down_left).astype(jnp.bfloat16)
    out_fwd = input_fwd.astype(jnp.float32) + product(hidden[:count_fwd], shared_down) + product(delta_out[:count_fwd], down_right)
    out_fwd = out_fwd.astype(jnp.bfloat16)
    hidden_bwd = hidden[count_fwd:]
    normed_bwd = normed[count_fwd:]
    din_bwd = delta_in[count_fwd:]
    dout_bwd = delta_out[count_fwd:]
    grad_down_right = product(dout_bwd.T, cotangent)
    grad_dout = product(cotangent, down_right.T).astype(jnp.bfloat16)
    grad_down_left = product(hidden_bwd.T, grad_dout)
    grad_hidden = product(cotangent, shared_down.T) + product(grad_dout, down_left.T)
    grad_preact = (grad_hidden * silu_slope(preact[count_fwd:])).astype(jnp.bfloat16)
    grad_up_right = product(din_bwd.T, grad_preact)
    grad_din = product(grad_preact, up_right.T).astype(jnp.bfloat16)
    grad_up_left = product(normed_bwd.T, grad_din)
    grad_normed = product(grad_preact, shared_up.T) + product(grad_din, up_left.T)
    grad_input = (cotangent.astype(jnp.float32) + grad_normed).astype(jnp.bfloat16)
    term_up = product(normed_bwd.T, grad_preact).astype(jnp.bfloat16).astype(jnp.float32)
    term_down = product(hidden_bwd.T, cotangent).astype(jnp.bfloat16).astype(jnp.float32)
    return out_fwd, grad_input, term_up, term_down, grad_up_left, grad_up_right, grad_down_left, grad_down_right


def reference(input_fwd, input_bwd, cotangent, shared_up, shared_down, up_left, up_right, down_left, down_right):
    def advance(totals, section_data):
        out_fwd, grad_input, term_up, term_down, g_ul, g_ur, g_dl, g_dr = one_section(shared_up, shared_down, section_data)
        totals = (totals[0] + term_up, totals[1] + term_down)
        return totals, (out_fwd, grad_input, g_ul, g_ur, g_dl, g_dr)

    start_totals = (jnp.zeros((D, FF), jnp.float32), jnp.zeros((FF, D), jnp.float32))
    totals, outputs = lax.scan(advance, start_totals, (input_fwd, input_bwd, cotangent, up_left, up_right, down_left, down_right))
    out_fwd, grad_input, g_ul, g_ur, g_dl, g_dr = outputs
    handoff_fwd = jnp.roll(out_fwd, 1, axis=0)
    handoff_bwd = jnp.roll(grad_input, -1, axis=0)
    grad_shared_up = totals[0].astype(jnp.bfloat16)
    grad_shared_down = totals[1].astype(jnp.bfloat16)
    return handoff_fwd, handoff_bwd, grad_shared_up, grad_shared_down, g_ul, g_ur, g_dl, g_dr
```

```python
import jax
import jax.numpy as jnp
import numpy as np
from jax import lax
from jax.sharding import PartitionSpec as P

F32 = jnp.float32
BF16 = jnp.bfloat16
PLACE = (2, 8, 2, 4, 2)
AXES = ("section", "row", "col")


def send(block, move):
    route = []
    for src in np.ndindex(*PLACE):
        dst = tuple(int(d) % n for d, n in zip(move(*src), PLACE))
        route.append((int(np.ravel_multi_index(src, PLACE)), int(np.ravel_multi_index(dst, PLACE))))
    return lax.ppermute(block, AXES, route)


def to_pair(block):
    return send(block, lambda a, z, r, y, k: (a + 1, z, r, y, k))


def to_row(block):
    return send(block, lambda a, z, r, y, k: (a, z, r + 1, y, k))


def to_core(block):
    return send(block, lambda a, z, r, y, k: (a, z, r, y, k + 1))


def to_y(block, hop):
    return send(block, lambda a, z, r, y, k: (a, z, r, y + hop, k))


def to_z(block, hop):
    return send(block, lambda a, z, r, y, k: (a, z + hop, r, y, k))


def to_section(block, hop):
    def move(a, z, r, y, k):
        s = (a * 8 + z + hop) % 16
        return (s // 8, s % 8, r, y, k)

    return send(block, move)


def pick(block, index, axis):
    return lax.dynamic_index_in_dim(block, index, axis, keepdims=False)


def turned(block, start):
    return lax.dynamic_slice_in_dim(jnp.concatenate([block, block], 0), start, 8, 0)


def mm(subscripts, left, right):
    return jnp.einsum(subscripts, left, right, preferred_element_type=F32)


def add(*terms):
    total = terms[0].astype(F32)
    for term in terms[1:]:
        total = total + term.astype(F32)
    return total


def ring_gather(block):
    ups, downs = [block], [block]
    for _ in range(4):
        ups.append(to_z(ups[-1], 1))
    for _ in range(3):
        downs.append(to_z(downs[-1], -1))
    return jnp.concatenate(ups[:0:-1] + downs, 0)


def ring_scatter(parts):
    plus = to_z(parts[0], 1)
    for i in (7, 6, 5):
        plus = to_z(add(plus, parts[i]).astype(BF16), 1)
    minus = to_z(parts[1], -1)
    for i in (2, 3):
        minus = to_z(add(minus, parts[i]).astype(BF16), -1)
    return add(parts[4], plus, minus)


def gather_tokens(block, part):
    mine = jnp.concatenate([block, part], 1)
    other = to_row(mine)
    both = jnp.concatenate([block, other[:, :1280], add(part, other[:, 1280:]).astype(BF16)], 1)
    both = jnp.stack([both, to_pair(both)])
    both = jnp.stack([both, to_y(both, 1), to_y(both, -1), to_y(both, 2)], 1)
    both = jnp.stack([both, to_core(both)], 1)
    both = both.reshape(2, 256, 2816)
    return both[:, :, :2560], both[:, :, 2560:]


def gather_own(block):
    both = jnp.stack([block, to_y(block, 1), to_y(block, -1), to_y(block, 2)])
    return jnp.concatenate([both, to_core(both)], 0).reshape(256, block.shape[-1])


def scatter_tokens(channels, rest):
    whole = jnp.concatenate([channels, rest], 2).astype(BF16)
    n = whole.shape[2]
    whole = whole.reshape(2, 2, 4, 32, n)
    whole = add(whole[:, 0], to_core(whole[:, 1])).astype(BF16)
    whole = add(
        whole[:, 0], to_y(whole[:, 1], -1), to_y(whole[:, 2], 1), to_y(whole[:, 3], 2)
    ).astype(BF16)
    whole = add(whole[0], to_pair(whole[1]))
    rounded = whole.astype(BF16)
    other = to_row(jnp.concatenate([rounded[:, 1280:2560], rounded[:, 2560:]], 1))
    return whole[:, :1280] + other[:, :1280].astype(F32), add(rounded[:, 2560:], other[:, 1280:])


def by_row(row, block):
    halves = block.reshape(2, 64, 1280)
    return jnp.concatenate([pick(halves, row, 0), to_row(pick(halves, 1 - row, 0))], 1)


def from_row(row, total):
    total = total.astype(BF16)
    mine, other = total[:, :1280], to_row(total[:, 1280:])
    first = jnp.where(row == 0, mine, other)
    second = jnp.where(row == 0, other, mine)
    return jnp.concatenate([first, second], 0)


def all_units(pair, z, row, block):
    half = jnp.stack([block[:, 0], to_pair(block[:, 1])])
    whole = jnp.stack([half, to_row(half)]).reshape(2, 2, 8, 64, 256)
    whole = jnp.where(row == 0, whole, whole[::-1])
    whole = jnp.where(pair == 0, whole, whole[:, ::-1])
    whole = jnp.transpose(whole, (2, 1, 0, 3, 4))
    whole = turned(whole, (12 - z) % 8)
    return jnp.transpose(whole, (1, 0, 2, 3, 4)).reshape(2048, 256)


def own_units(pair, z, row, factor):
    units = pick(factor.reshape(2, 8, 2, 64, 256), row, 2)
    mine, other = pick(units, pair, 0), pick(units, 1 - pair, 0)
    mine, other = turned(mine, (z + 4) % 8), turned(other, (z + 4) % 8)
    return jnp.stack([mine.reshape(512, 256), to_pair(other.reshape(512, 256))])


def local(
    input_fwd,
    input_bwd,
    cotangent,
    shared_up,
    shared_down,
    up_left,
    up_right,
    down_left,
    down_right,
):
    section, row = lax.axis_index("section"), lax.axis_index("row")
    pair, z = section // 8, section % 8
    in_fwd, in_bwd, cot = input_fwd[0], input_bwd[0], cotangent[0]
    in_left, out_right = up_left[0], down_right[0]

    up0 = by_row(row, shared_up.T)
    down0 = by_row(row, shared_down)
    x_bwd, din_bwd = gather_tokens(in_bwd, mm("td,dr->tr", in_bwd, in_left).astype(BF16))
    up = ring_gather(up0)
    in_right = own_units(pair, z, row, up_right[0].T)
    cots, gdout = gather_tokens(cot, mm("td,rd->tr", cot, out_right).astype(BF16))
    down = ring_gather(down0)
    out_left = own_units(pair, z, row, down_left[0])
    x_fwd, din_fwd = gather_tokens(in_fwd, mm("td,dr->tr", in_fwd, in_left).astype(BF16))

    pre_bwd = mm("fd,std->fst", up, x_bwd) + mm("sfr,str->fst", in_right, din_bwd)
    sigma = jax.nn.sigmoid(pre_bwd)
    hid_bwd = (pre_bwd * sigma).astype(BF16)
    slope = sigma * (1.0 + pre_bwd * (1.0 - sigma))
    grad_down = mm("fst,std->fd", hid_bwd, cots).astype(BF16).reshape(8, 64, 2560)
    sum_down = ring_scatter(grad_down)
    grad_hid = mm("fd,std->fst", down, cots) + mm("sfr,str->fst", out_left, gdout)
    grad_pre = (grad_hid * slope).astype(BF16)
    grad_up = mm("fst,std->fd", grad_pre, x_bwd).astype(BF16).reshape(8, 64, 2560)
    sum_up = ring_scatter(grad_up)

    pre_fwd = mm("fd,std->fst", up, x_fwd) + mm("sfr,str->fst", in_right, din_fwd)
    hid_fwd = jax.nn.silu(pre_fwd).astype(BF16)
    out_part = mm("fst,fd->std", hid_fwd, down)
    dout_part = jnp.concatenate(
        [mm("fst,sfr->str", hid_fwd, out_left), mm("fst,sfr->str", hid_bwd, out_left)], 2
    )
    down_own, dout_own = scatter_tokens(out_part, dout_part)
    dout_own = dout_own.astype(BF16)
    out_fwd = in_fwd.astype(F32) + down_own + mm("tr,rd->td", dout_own[:, :256], out_right)
    handoff_fwd = to_section(out_fwd.astype(BF16), 1)

    norm_part = mm("fst,fd->std", grad_pre, up)
    gdin_part = mm("fst,sfr->str", grad_pre, in_right)
    norm_own, gdin_own = scatter_tokens(norm_part, gdin_part)
    gdin_own = gdin_own.astype(BF16)
    grad_in = cot.astype(F32) + norm_own + mm("tr,dr->td", gdin_own, in_left)
    handoff_bwd = to_section(grad_in.astype(BF16), -1)

    own_all = gather_own(jnp.concatenate([dout_own[:, 256:], gdin_own], 1))
    grad_down_right = mm("tr,td->rd", own_all[:, :256], cots[0, :, :1280])
    grad_up_left = mm("td,tr->dr", x_bwd[0, :, :1280], own_all[:, 256:])
    grad_down_left = mm("ft,tr->fr", all_units(pair, z, row, hid_bwd), gdout[0])
    grad_up_right = mm("tr,ft->rf", din_bwd[0], all_units(pair, z, row, grad_pre))
    return (
        handoff_fwd[None],
        handoff_bwd[None],
        from_row(row, sum_up).T,
        from_row(row, sum_down),
        grad_up_left[None],
        grad_up_right[None],
        grad_down_left[None],
        grad_down_right[None],
    )


def solution(mesh):
    in_specs = (
        P("section", "col", "row"),
        P("section", "col", "row"),
        P("section", "col", "row"),
        P("row", ("col", "section")),
        P(("col", "section"), "row"),
        P("section", "row", None),
        P("section", None, "col"),
        P("section", "col", None),
        P("section", None, "row"),
    )
    out_specs = (
        P("section", "col", "row"),
        P("section", "col", "row"),
        P("row", ("col", "section")),
        P(("col", "section"), "row"),
        P("section", "row", None),
        P("section", None, "col"),
        P("section", "col", None),
        P("section", None, "row"),
    )
    return jax.shard_map(local, mesh=mesh, in_specs=in_specs, out_specs=out_specs, check_vma=False)
```

```python
import jax
import jax.numpy as jnp
import numpy as np
from jax import lax
from jax.sharding import PartitionSpec as P

F32 = jnp.float32
BF16 = jnp.bfloat16
PLACE = (2, 8, 2, 4, 2)
AXES = ("section", "row", "col")


def send(block, move):
    route = []
    for src in np.ndindex(*PLACE):
        dst = tuple(int(d) % n for d, n in zip(move(*src), PLACE))
        route.append((int(np.ravel_multi_index(src, PLACE)), int(np.ravel_multi_index(dst, PLACE))))
    return lax.ppermute(block, AXES, route)


def to_pair(block):
    return send(block, lambda a, z, r, y, k: (a + 1, z, r, y, k))


def to_row(block):
    return send(block, lambda a, z, r, y, k: (a, z, r + 1, y, k))


def to_core(block):
    return send(block, lambda a, z, r, y, k: (a, z, r, y, k + 1))


def to_y(block, hop):
    return send(block, lambda a, z, r, y, k: (a, z, r, y + hop, k))


def to_z(block, hop):
    return send(block, lambda a, z, r, y, k: (a, z + hop, r, y, k))


def to_section(block, hop):
    def move(a, z, r, y, k):
        s = (a * 8 + z + hop) % 16
        return (s // 8, s % 8, r, y, k)

    return send(block, move)


def pick(block, index, axis):
    return lax.dynamic_index_in_dim(block, index, axis, keepdims=False)


def turned(block, start):
    return lax.dynamic_slice_in_dim(jnp.concatenate([block, block], 0), start, 8, 0)


def mm(subscripts, left, right):
    return jnp.einsum(subscripts, left, right, preferred_element_type=F32)


def add(*terms):
    total = terms[0].astype(F32)
    for term in terms[1:]:
        total = total + term.astype(F32)
    return total


def together(*blocks):
    return lax.optimization_barrier(blocks)


def tokens_first(block, part):
    return jnp.concatenate([block, part], -1)


def all_channels(mine, other):
    return jnp.concatenate(
        [mine[..., :1280], other[..., :1280], add(mine[..., 1280:], other[..., 1280:]).astype(BF16)], -1
    )


def scatter_y(block):
    sent = (to_y(block[1], -1), to_y(block[2], 1), to_y(block[3], 2))
    return lambda *got: add(block[0], *got).astype(BF16), sent


def from_row(row, mine, other):
    first = jnp.where(row == 0, mine, other)
    second = jnp.where(row == 0, other, mine)
    return jnp.concatenate([first, second], 0)


def in_order(pair, z, row, half, other):
    whole = jnp.stack([half, other]).reshape(2, 2, 8, 64, 256)
    whole = jnp.where(row == 0, whole, whole[::-1])
    whole = jnp.where(pair == 0, whole, whole[:, ::-1])
    whole = jnp.transpose(whole, (2, 1, 0, 3, 4))
    whole = turned(whole, (12 - z) % 8)
    return jnp.transpose(whole, (1, 0, 2, 3, 4)).reshape(2048, 256)


def own_units(pair, z, row, factor):
    units = pick(factor.reshape(2, 8, 2, 64, 256), row, 2)
    mine, other = pick(units, pair, 0), pick(units, 1 - pair, 0)
    mine, other = turned(mine, (z + 4) % 8), turned(other, (z + 4) % 8)
    return mine.reshape(512, 256), other.reshape(512, 256)


def local(
    input_fwd,
    input_bwd,
    cotangent,
    shared_up,
    shared_down,
    up_left,
    up_right,
    down_left,
    down_right,
):
    section, row = lax.axis_index("section"), lax.axis_index("row")
    pair, z = section // 8, section % 8
    in_fwd, in_bwd, cot = input_fwd[0], input_bwd[0], cotangent[0]
    in_left, out_right = up_left[0], down_right[0]

    halves = jnp.stack([shared_up.T, shared_down]).reshape(2, 2, 64, 1280)
    mine_w = pick(halves, row, 1)
    got_w = to_row(pick(halves, 1 - row, 1))

    fwd = tokens_first(in_fwd, mm("td,dr->tr", in_fwd, in_left).astype(BF16))
    bwd = jnp.concatenate(
        [
            tokens_first(in_bwd, mm("td,dr->tr", in_bwd, in_left).astype(BF16)),
            tokens_first(cot, mm("td,rd->tr", cot, out_right).astype(BF16)),
        ],
        0,
    )
    got_bwd = to_row(bwd)
    fwd_y = (to_y(fwd, 1), to_y(fwd, -1), to_y(fwd, 2))
    got_w, got_bwd = together(got_w, got_bwd)

    w0 = jnp.concatenate([mine_w, got_w], 2)
    bwd = all_channels(bwd, got_bwd)
    plus1, minus1 = to_z(w0, 1), to_z(w0, -1)
    pair_bwd = to_pair(bwd)
    plus1, minus1, pair_bwd, *fwd_y = together(plus1, minus1, pair_bwd, *fwd_y)

    plus2, minus2 = to_z(plus1, 1), to_z(minus1, -1)
    bwd = jnp.stack([bwd, pair_bwd])
    bwd_y = (to_y(bwd, 1), to_y(bwd, -1), to_y(bwd, 2))
    fwd = jnp.stack([fwd, *fwd_y])
    got_fwd = to_row(fwd)
    plus2, minus2, got_fwd = together(plus2, minus2, got_fwd)

    plus3, minus3 = to_z(plus2, 1), to_z(minus2, -1)
    fwd = all_channels(fwd, got_fwd)
    pair_fwd = to_pair(fwd)
    plus3, minus3, pair_fwd, *bwd_y = together(plus3, minus3, pair_fwd, *bwd_y)

    far_up, far_down = to_z(plus3[0], 1), to_z(minus3[1], -1)
    bwd = jnp.stack([bwd, *bwd_y], 1)
    core_bwd = to_core(bwd)
    fwd = jnp.stack([fwd, pair_fwd])
    core_fwd = to_core(fwd)
    right_own, right_other = own_units(pair, z, row, up_right[0].T)
    left_own, left_other = own_units(pair, z, row, down_left[0])
    got_units = to_pair(jnp.stack([right_other, left_other]))
    in_right = jnp.stack([right_own, got_units[0]])
    out_left = jnp.stack([left_own, got_units[1]])
    up = jnp.concatenate([far_up, plus3[0], plus2[0], plus1[0], w0[0], minus1[0], minus2[0], minus3[0]], 0)
    down = jnp.concatenate([far_down, plus3[1], plus2[1], plus1[1], w0[1], minus1[1], minus2[1], minus3[1]], 0)
    bwd = jnp.stack([bwd, core_bwd], 1)
    x_bwd, cots = bwd[:, :, :, :32].reshape(2, 256, 2816), bwd[:, :, :, 32:].reshape(2, 256, 2816)
    x_fwd = jnp.stack([fwd, core_fwd], 1).reshape(2, 256, 2816)
    x_bwd, din_bwd = x_bwd[:, :, :2560], x_bwd[:, :, 2560:]
    cots, gdout = cots[:, :, :2560], cots[:, :, 2560:]
    x_fwd, din_fwd = x_fwd[:, :, :2560], x_fwd[:, :, 2560:]

    pre_bwd = mm("fd,std->fst", up, x_bwd) + mm("sfr,str->fst", in_right, din_bwd)
    sigma = jax.nn.sigmoid(pre_bwd)
    hid_bwd = (pre_bwd * sigma).astype(BF16)
    slope = sigma * (1.0 + pre_bwd * (1.0 - sigma))
    grad_hid = mm("fd,std->fst", down, cots) + mm("sfr,str->fst", out_left, gdout)
    grad_pre = (grad_hid * slope).astype(BF16)
    gdown = mm("fst,std->fd", hid_bwd, cots).astype(BF16).reshape(8, 64, 2560)
    gup = mm("fst,std->fd", grad_pre, x_bwd).astype(BF16).reshape(8, 64, 2560)

    far_up, far_down = to_z(gup[0], 1), to_z(gdown[0], -1)
    norm_part = mm("fst,fd->std", grad_pre, up)
    gdin_part = mm("fst,sfr->str", grad_pre, in_right)
    send_n = jnp.concatenate([norm_part, gdin_part], 2).astype(BF16).reshape(2, 2, 4, 32, 2816)
    core_n = to_core(send_n[:, 1])
    units = jnp.stack([hid_bwd, grad_pre])
    pair_units = to_pair(units[:, :, 1])
    far_up, far_down, core_n = together(far_up, far_down, core_n)

    plus = to_z(jnp.stack([add(far_up, gup[7]).astype(BF16), gdown[7]]), 1)
    minus = to_z(jnp.stack([gup[1], add(far_down, gdown[1]).astype(BF16)]), -1)
    sum_n = add(send_n[:, 0], core_n).astype(BF16)
    pair_n = to_pair(sum_n[1])
    pre_fwd = mm("fd,std->fst", up, x_fwd) + mm("sfr,str->fst", in_right, din_fwd)
    hid_fwd = jax.nn.silu(pre_fwd).astype(BF16)
    send_f = jnp.concatenate(
        [
            mm("fst,fd->std", hid_fwd, down),
            mm("fst,sfr->str", hid_fwd, out_left),
            mm("fst,sfr->str", hid_bwd, out_left),
        ],
        2,
    )
    send_f = send_f.astype(BF16).reshape(2, 2, 4, 32, 3072)
    core_f = to_core(send_f[:, 1])
    plus, minus, pair_n, core_f, pair_units = together(plus, minus, pair_n, core_f, pair_units)

    plus = to_z(jnp.stack([add(plus[0], gup[6]), add(plus[1], gdown[6])]).astype(BF16), 1)
    minus = to_z(jnp.stack([add(minus[0], gup[2]), add(minus[1], gdown[2])]).astype(BF16), -1)
    sum_n = add(sum_n[0], pair_n).astype(BF16)
    total_n, sent_n = scatter_y(sum_n)
    sum_f = add(send_f[:, 0], core_f).astype(BF16)
    pair_f = to_pair(sum_f[1])
    half_units = jnp.stack([units[:, :, 0], pair_units], 1)
    other_units = to_row(half_units)
    plus, minus, pair_f, *sent_n = together(plus, minus, pair_f, *sent_n)

    plus = to_z(jnp.stack([add(plus[0], gup[5]), add(plus[1], gdown[5])]).astype(BF16), 1)
    minus = to_z(jnp.stack([add(minus[0], gup[3]), add(minus[1], gdown[3])]).astype(BF16), -1)
    sum_n = total_n(*sent_n)
    row_n = to_row(sum_n[:, 1280:])
    sum_f = add(sum_f[0], pair_f).astype(BF16)
    total_f, sent_f = scatter_y(sum_f)
    sum_f = total_f(*sent_f)
    row_f = to_row(sum_f[:, 1280:])
    plus, minus, row_n, row_f, other_units = together(plus, minus, row_n, row_f, other_units)

    total = add(jnp.stack([gup[4], gdown[4]]), plus, minus).astype(BF16)
    got = to_row(total[:, :, 1280:])
    gdin_own = add(sum_n[:, 2560:], row_n[:, 1280:]).astype(BF16)
    dout_own = add(sum_f[:, 2560:], row_f[:, 1280:]).astype(BF16)
    grad_in = add(cot, sum_n[:, :1280], row_n[:, :1280]) + mm("tr,dr->td", gdin_own, in_left)
    handoff_bwd = to_section(grad_in.astype(BF16), -1)
    out_fwd = add(in_fwd, sum_f[:, :1280], row_f[:, :1280]) + mm("tr,rd->td", dout_own[:, :256], out_right)
    handoff_fwd = to_section(out_fwd.astype(BF16), 1)
    own = jnp.concatenate([dout_own[:, 256:], gdin_own], 1)
    own = jnp.stack([own, to_y(own, 1), to_y(own, -1), to_y(own, 2)])
    own_all = jnp.concatenate([own, to_core(own)], 0).reshape(256, 512)
    grad_down_right = mm("tr,td->rd", own_all[:, :256], cots[0, :, :1280])
    grad_up_left = mm("td,tr->dr", x_bwd[0, :, :1280], own_all[:, 256:])
    hid_all = in_order(pair, z, row, half_units[0], other_units[0])
    pre_all = in_order(pair, z, row, half_units[1], other_units[1])
    grad_down_left = mm("ft,tr->fr", hid_all, gdout[0])
    grad_up_right = mm("tr,ft->rf", din_bwd[0], pre_all)
    return (
        handoff_fwd[None],
        handoff_bwd[None],
        from_row(row, total[0, :, :1280], got[0]).T,
        from_row(row, total[1, :, :1280], got[1]),
        grad_up_left[None],
        grad_up_right[None],
        grad_down_left[None],
        grad_down_right[None],
    )


def solution(mesh):
    in_specs = (
        P("section", "col", "row"),
        P("section", "col", "row"),
        P("section", "col", "row"),
        P("row", ("col", "section")),
        P(("col", "section"), "row"),
        P("section", "row", None),
        P("section", None, "col"),
        P("section", "col", None),
        P("section", None, "row"),
    )
    out_specs = (
        P("section", "col", "row"),
        P("section", "col", "row"),
        P("row", ("col", "section")),
        P(("col", "section"), "row"),
        P("section", "row", None),
        P("section", None, "col"),
        P("section", "col", None),
        P("section", None, "row"),
    )
    return jax.shard_map(local, mesh=mesh, in_specs=in_specs, out_specs=out_specs, check_vma=False)
```

```python
import jax
import jax.numpy as jnp
import numpy as np
from jax import lax
from jax.sharding import PartitionSpec as P

F32 = jnp.float32
BF16 = jnp.bfloat16
PLACE = (2, 8, 2, 4, 2)
AXES = ("section", "row", "col")


def send(block, move):
    route = []
    for src in np.ndindex(*PLACE):
        dst = tuple(int(d) % n for d, n in zip(move(*src), PLACE))
        route.append((int(np.ravel_multi_index(src, PLACE)), int(np.ravel_multi_index(dst, PLACE))))
    return lax.ppermute(block, AXES, route)


def to_pair(block):
    return send(block, lambda a, z, r, y, k: (a + 1, z, r, y, k))


def to_row(block):
    return send(block, lambda a, z, r, y, k: (a, z, r + 1, y, k))


def to_core(block):
    return send(block, lambda a, z, r, y, k: (a, z, r, y, k + 1))


def to_y(block, hop):
    return send(block, lambda a, z, r, y, k: (a, z, r, y + hop, k))


def to_z(block, hop):
    return send(block, lambda a, z, r, y, k: (a, z + hop, r, y, k))


def to_section(block, hop):
    def move(a, z, r, y, k):
        s = (a * 8 + z + hop) % 16
        return (s // 8, s % 8, r, y, k)

    return send(block, move)


def pick(block, index, axis):
    return lax.dynamic_index_in_dim(block, index, axis, keepdims=False)


def turned(block, start):
    return lax.dynamic_slice_in_dim(jnp.concatenate([block, block], 0), start, 8, 0)


def mm(subscripts, left, right):
    return jnp.einsum(subscripts, left, right, preferred_element_type=F32)


def add(*terms):
    total = terms[0].astype(F32)
    for term in terms[1:]:
        total = total + term.astype(F32)
    return total


def together(*blocks):
    return lax.optimization_barrier(blocks)


def tokens_first(block, part):
    return jnp.concatenate([block, part], -1)


def all_channels(mine, other):
    return jnp.concatenate(
        [mine[..., :1280], other[..., :1280], add(mine[..., 1280:], other[..., 1280:]).astype(BF16)], -1
    )


def scatter_y(block):
    sent = (to_y(block[1], -1), to_y(block[2], 1), to_y(block[3], 2))
    return lambda *got: add(block[0], *got).astype(BF16), sent


def from_row(row, mine, other):
    first = jnp.where(row == 0, mine, other)
    second = jnp.where(row == 0, other, mine)
    return jnp.concatenate([first, second], 0)


def in_order(pair, z, row, half, other):
    whole = jnp.stack([half, other]).reshape(2, 2, 8, 64, 256)
    whole = jnp.where(row == 0, whole, whole[::-1])
    whole = jnp.where(pair == 0, whole, whole[:, ::-1])
    whole = jnp.transpose(whole, (2, 1, 0, 3, 4))
    whole = turned(whole, (12 - z) % 8)
    return jnp.transpose(whole, (1, 0, 2, 3, 4)).reshape(2048, 256)


def own_units(pair, z, row, factor):
    units = pick(factor.reshape(2, 8, 2, 64, 256), row, 2)
    mine, other = pick(units, pair, 0), pick(units, 1 - pair, 0)
    mine, other = turned(mine, (z + 4) % 8), turned(other, (z + 4) % 8)
    return mine.reshape(512, 256), other.reshape(512, 256)


def local(
    input_fwd,
    input_bwd,
    cotangent,
    shared_up,
    shared_down,
    up_left,
    up_right,
    down_left,
    down_right,
):
    section, row = lax.axis_index("section"), lax.axis_index("row")
    pair, z = section // 8, section % 8
    in_fwd, in_bwd, cot = input_fwd[0], input_bwd[0], cotangent[0]
    in_left, out_right = up_left[0], down_right[0]

    halves = jnp.stack([shared_up.T, shared_down]).reshape(2, 2, 64, 1280)
    own = [pick(halves, row, 1)]
    far = to_row(pick(halves, 1 - row, 1))
    own += [to_z(own[0], 1), to_z(own[0], -1)]

    bwd = jnp.concatenate(
        [
            tokens_first(in_bwd, mm("td,dr->tr", in_bwd, in_left).astype(BF16)),
            tokens_first(cot, mm("td,rd->tr", cot, out_right).astype(BF16)),
        ],
        0,
    )
    got_bwd = to_row(bwd)
    fwd = tokens_first(in_fwd, mm("td,dr->tr", in_fwd, in_left).astype(BF16))
    fwd_y = (to_y(fwd, 1), to_y(fwd, -1), to_y(fwd, 2))

    far, got_bwd = together(far, got_bwd)
    far = [far, to_z(far, 1), to_z(far, -1)]
    bwd = all_channels(bwd, got_bwd)
    pair_bwd = to_pair(bwd)

    own[1], own[2], pair_bwd, *fwd_y = together(own[1], own[2], pair_bwd, *fwd_y)
    own += [to_z(own[1], 1), to_z(own[2], -1)]
    bwd = jnp.stack([bwd, pair_bwd])
    bwd_y = (to_y(bwd, 1), to_y(bwd, -1), to_y(bwd, 2))
    fwd = jnp.stack([fwd, *fwd_y])
    got_fwd = to_row(fwd)

    far[1], far[2], got_fwd = together(far[1], far[2], got_fwd)
    far += [to_z(far[1], 1), to_z(far[2], -1)]
    fwd = all_channels(fwd, got_fwd)
    pair_fwd = to_pair(fwd)

    own[3], own[4] = together(own[3], own[4])
    own += [to_z(own[3], 1), to_z(own[4], -1)]

    far[3], far[4], pair_fwd = together(far[3], far[4], pair_fwd)
    far += [to_z(far[3], 1), to_z(far[4], -1)]
    fwd = jnp.stack([fwd, pair_fwd])
    core_fwd = to_core(fwd)
    right_own, right_other = own_units(pair, z, row, up_right[0].T)
    left_own, left_other = own_units(pair, z, row, down_left[0])
    got_units = to_pair(jnp.stack([right_other, left_other]))

    own[5], own[6], *bwd_y = together(own[5], own[6], *bwd_y)
    own_last = (to_z(own[5][0], 1), to_z(own[6][1], -1))
    bwd = jnp.stack([bwd, *bwd_y], 1)
    core_bwd = to_core(bwd)

    far[5], far[6], got_units = together(far[5], far[6], got_units)
    far_last = (to_z(far[5][0], 1), to_z(far[6][1], -1))
    order = (5, 3, 1, 0, 2, 4, 6)

    in_right = jnp.stack([right_own, got_units[0]])
    out_left = jnp.stack([left_own, got_units[1]])
    bwd = jnp.stack([bwd, core_bwd], 1)
    x_bwd, cots = bwd[:, :, :, :32].reshape(2, 256, 2816), bwd[:, :, :, 32:].reshape(2, 256, 2816)
    x_fwd = jnp.stack([fwd, core_fwd], 1).reshape(2, 256, 2816)
    x_bwd, din_bwd = x_bwd[:, :, :2560], x_bwd[:, :, 2560:]
    cots, gdout = cots[:, :, :2560], cots[:, :, 2560:]
    x_fwd, din_fwd = x_fwd[:, :, :2560], x_fwd[:, :, 2560:]

    def backward(up, down, in_right, out_left):
        pre = mm("fd,std->fst", up, x_bwd) + mm("sfr,str->fst", in_right, din_bwd)
        sigma = jax.nn.sigmoid(pre)
        hid = (pre * sigma).astype(BF16)
        slope = sigma * (1.0 + pre * (1.0 - sigma))
        grad_hid = mm("fd,std->fst", down, cots) + mm("sfr,str->fst", out_left, gdout)
        grad_pre = (grad_hid * slope).astype(BF16)
        gdown = mm("fst,std->fd", hid, cots).astype(BF16).reshape(-1, 64, 2560)
        gup = mm("fst,std->fd", grad_pre, x_bwd).astype(BF16).reshape(-1, 64, 2560)
        return hid, grad_pre, gup, gdown

    near = [
        jnp.concatenate([jnp.concatenate([own[i][w], far[i][w]], 1) for i in order], 0) for w in range(2)
    ]
    hid1, pre1, gup1, gdown1 = backward(near[0], near[1], in_right[:, 64:], out_left[:, 64:])

    own_last, far_last, gup1, gdown1 = together(own_last, far_last, gup1, gdown1)
    last = [jnp.concatenate([own_last[w], far_last[w]], 1) for w in range(2)]
    hid0, pre0, gup0, gdown0 = backward(last[0], last[1], in_right[:, :64], out_left[:, :64])

    gup, gdown = jnp.concatenate([gup0, gup1], 0), jnp.concatenate([gdown0, gdown1], 0)
    gup_far, gdown_far, gup_own, gdown_own = gup[:, :, 1280:], gdown[:, :, 1280:], gup[:, :, :1280], gdown[:, :, :1280]

    def first(up, down):
        return to_z(up[0], 1), to_z(down[0], -1)

    def second(up, down, got):
        plus = jnp.stack([add(got[0], up[7]).astype(BF16), down[7]])
        minus = jnp.stack([up[1], add(got[1], down[1]).astype(BF16)])
        return to_z(plus, 1), to_z(minus, -1)

    def following(up, down, got, i, j):
        plus = jnp.stack([add(got[0][0], up[i]), add(got[0][1], down[i])]).astype(BF16)
        minus = jnp.stack([add(got[1][0], up[j]), add(got[1][1], down[j])]).astype(BF16)
        return to_z(plus, 1), to_z(minus, -1)

    def final(up, down, got):
        return add(jnp.stack([up[4], down[4]]), *got).astype(BF16)

    sum_far = first(gup0[:, :, 1280:], gdown0[:, :, 1280:])
    sum_own = first(gup0[:, :, :1280], gdown0[:, :, :1280])
    hid_bwd, grad_pre = jnp.concatenate([hid0, hid1], 0), jnp.concatenate([pre0, pre1], 0)
    units = jnp.stack([hid_bwd, grad_pre])
    pair_units = to_pair(units[:, :, 1])
    up, down = jnp.concatenate([last[0], near[0]], 0), jnp.concatenate([last[1], near[1]], 0)
    send_n = jnp.concatenate(
        [mm("fst,fd->std", grad_pre, up), mm("fst,sfr->str", grad_pre, in_right)], 2
    )
    send_n = send_n.astype(BF16).reshape(2, 2, 4, 32, 2816)
    core_n = to_core(send_n[:, 1])

    sum_far = together(*sum_far)
    sum_far = second(gup_far, gdown_far, sum_far)
    *sum_own, core_n = together(*sum_own, core_n)
    sum_own = second(gup_own, gdown_own, sum_own)
    total_n, sent_n = scatter_y(jnp.moveaxis(add(send_n[:, 0], core_n).astype(BF16), 1, 0))
    pre_fwd = mm("fd,std->fst", up, x_fwd) + mm("sfr,str->fst", in_right, din_fwd)
    hid_fwd = jax.nn.silu(pre_fwd).astype(BF16)
    send_f = jnp.concatenate(
        [
            mm("fst,fd->std", hid_fwd, down),
            mm("fst,sfr->str", hid_fwd, out_left),
            mm("fst,sfr->str", hid_bwd, out_left),
        ],
        2,
    )
    send_f = send_f.astype(BF16).reshape(2, 2, 4, 32, 3072)
    core_f = to_core(send_f[:, 1])

    *sum_far, pair_units = together(*sum_far, pair_units)
    sum_far = following(gup_far, gdown_far, sum_far, 6, 2)
    half_units = jnp.stack([units[:, :, 0], pair_units], 1)
    other_units = to_row(half_units)
    *sum_own, core_f, a0, a1, a2 = together(*sum_own, core_f, *sent_n)
    sent_n = (a0, a1, a2)
    sum_own = following(gup_own, gdown_own, sum_own, 6, 2)
    total_f, sent_f = scatter_y(jnp.moveaxis(add(send_f[:, 0], core_f).astype(BF16), 1, 0))
    sum_n = total_n(*sent_n)
    pair_n = to_pair(sum_n[1])

    *sum_far, pair_n = together(*sum_far, pair_n)
    sum_far = following(gup_far, gdown_far, sum_far, 5, 3)
    sum_n = add(sum_n[0], pair_n).astype(BF16)
    row_n = to_row(sum_n[:, 1280:])
    *sum_own, a0, a1, a2 = together(*sum_own, *sent_f)
    sent_f = (a0, a1, a2)
    sum_own = following(gup_own, gdown_own, sum_own, 5, 3)
    sum_f = total_f(*sent_f)
    pair_f = to_pair(sum_f[1])

    *sum_far, row_n, other_units = together(*sum_far, row_n, other_units)
    got = to_row(final(gup_far, gdown_far, sum_far))
    gdin_own = add(sum_n[:, 2560:], row_n[:, 1280:]).astype(BF16)
    grad_in = add(cot, sum_n[:, :1280], row_n[:, :1280]) + mm("tr,dr->td", gdin_own, in_left)
    handoff_bwd = to_section(grad_in.astype(BF16), -1)
    sum_f = add(sum_f[0], pair_f).astype(BF16)
    row_f = to_row(sum_f[:, 1280:])
    hid_all = in_order(pair, z, row, half_units[0], other_units[0])
    pre_all = in_order(pair, z, row, half_units[1], other_units[1])
    grad_down_left = mm("ft,tr->fr", hid_all, gdout[0])
    grad_up_right = mm("tr,ft->rf", din_bwd[0], pre_all)

    dout_own = add(sum_f[:, 2560:], row_f[:, 1280:]).astype(BF16)
    out_fwd = add(in_fwd, sum_f[:, :1280], row_f[:, :1280]) + mm("tr,rd->td", dout_own[:, :256], out_right)
    handoff_fwd = to_section(out_fwd.astype(BF16), 1)
    rest = jnp.concatenate([dout_own[:, 256:], gdin_own], 1)
    rest = jnp.stack([rest, to_y(rest, 1), to_y(rest, -1), to_y(rest, 2)])
    rest = jnp.concatenate([rest, to_core(rest)], 0).reshape(256, 512)
    grad_down_right = mm("tr,td->rd", rest[:, :256], cots[0, :, :1280])
    grad_up_left = mm("td,tr->dr", x_bwd[0, :, :1280], rest[:, 256:])
    total = final(gup_own, gdown_own, sum_own)
    return (
        handoff_fwd[None],
        handoff_bwd[None],
        from_row(row, total[0], got[0]).T,
        from_row(row, total[1], got[1]),
        grad_up_left[None],
        grad_up_right[None],
        grad_down_left[None],
        grad_down_right[None],
    )


def solution(mesh):
    in_specs = (
        P("section", "col", "row"),
        P("section", "col", "row"),
        P("section", "col", "row"),
        P("row", ("col", "section")),
        P(("col", "section"), "row"),
        P("section", "row", None),
        P("section", None, "col"),
        P("section", "col", None),
        P("section", None, "row"),
    )
    out_specs = (
        P("section", "col", "row"),
        P("section", "col", "row"),
        P("row", ("col", "section")),
        P(("col", "section"), "row"),
        P("section", "row", None),
        P("section", None, "col"),
        P("section", "col", None),
        P("section", None, "row"),
    )
    return jax.shard_map(local, mesh=mesh, in_specs=in_specs, out_specs=out_specs, check_vma=False)
```

```python
import jax
import jax.numpy as jnp
import numpy as np
from jax import lax
from jax.sharding import PartitionSpec as P

F32 = jnp.float32
BF16 = jnp.bfloat16
PLACE = (2, 8, 2, 4, 2)
AXES = ("section", "row", "col")


def send(block, move):
    route = []
    for src in np.ndindex(*PLACE):
        dst = tuple(int(d) % n for d, n in zip(move(*src), PLACE))
        route.append((int(np.ravel_multi_index(src, PLACE)), int(np.ravel_multi_index(dst, PLACE))))
    return lax.ppermute(block, AXES, route)


def to_pair(block):
    return send(block, lambda a, z, r, y, k: (a + 1, z, r, y, k))


def to_row(block):
    return send(block, lambda a, z, r, y, k: (a, z, r + 1, y, k))


def to_core(block):
    return send(block, lambda a, z, r, y, k: (a, z, r, y, k + 1))


def to_y(block, hop):
    return send(block, lambda a, z, r, y, k: (a, z, r, y + hop, k))


def to_z(block, hop):
    return send(block, lambda a, z, r, y, k: (a, z + hop, r, y, k))


def to_section(block, hop):
    def move(a, z, r, y, k):
        s = (a * 8 + z + hop) % 16
        return (s // 8, s % 8, r, y, k)

    return send(block, move)


def pick(block, index, axis):
    return lax.dynamic_index_in_dim(block, index, axis, keepdims=False)


def turned(block, start):
    return lax.dynamic_slice_in_dim(jnp.concatenate([block, block], 0), start, 8, 0)


def mm(subscripts, left, right):
    return jnp.einsum(subscripts, left, right, preferred_element_type=F32)


def add(*terms):
    total = terms[0].astype(F32)
    for term in terms[1:]:
        total = total + term.astype(F32)
    return total


def together(*blocks):
    return lax.optimization_barrier(blocks)


def tokens_first(block, part):
    return jnp.concatenate([block, part], -1)


def all_channels(mine, other):
    return jnp.concatenate(
        [mine[..., :1280], other[..., :1280], add(mine[..., 1280:], other[..., 1280:]).astype(BF16)], -1
    )


def scatter_y(block):
    sent = (to_y(block[1], -1), to_y(block[2], 1), to_y(block[3], 2))
    return lambda *got: add(block[0], *got).astype(BF16), sent


def from_row(row, mine, other):
    first = jnp.where(row == 0, mine, other)
    second = jnp.where(row == 0, other, mine)
    return jnp.concatenate([first, second], 0)


def in_order(pair, z, row, half, other):
    whole = jnp.stack([half, other]).reshape(2, 2, 8, 64, 256)
    whole = jnp.where(row == 0, whole, whole[::-1])
    whole = jnp.where(pair == 0, whole, whole[:, ::-1])
    whole = jnp.transpose(whole, (2, 1, 0, 3, 4))
    whole = turned(whole, (12 - z) % 8)
    return jnp.transpose(whole, (1, 0, 2, 3, 4)).reshape(2048, 256)


def own_units(pair, z, row, factor):
    units = pick(factor.reshape(2, 8, 2, 64, 256), row, 2)
    mine, other = pick(units, pair, 0), pick(units, 1 - pair, 0)
    mine, other = turned(mine, (z + 4) % 8), turned(other, (z + 4) % 8)
    return mine.reshape(512, 256), other.reshape(512, 256)


def local(
    input_fwd,
    input_bwd,
    cotangent,
    shared_up,
    shared_down,
    up_left,
    up_right,
    down_left,
    down_right,
):
    section, row = lax.axis_index("section"), lax.axis_index("row")
    pair, z = section // 8, section % 8
    in_fwd, in_bwd, cot = input_fwd[0], input_bwd[0], cotangent[0]
    in_left, out_right = up_left[0], down_right[0]

    halves = jnp.stack([shared_up.T, shared_down]).reshape(2, 2, 64, 1280)
    mine_w = pick(halves, row, 1)
    give_w = pick(halves, 1 - row, 1)
    got_w = to_row(give_w)
    give_w, in_fwd, in_bwd, cot = together(give_w, in_fwd, in_bwd, cot)

    fwd = tokens_first(in_fwd, mm("td,dr->tr", in_fwd, in_left).astype(BF16))
    bwd = jnp.concatenate(
        [
            tokens_first(in_bwd, mm("td,dr->tr", in_bwd, in_left).astype(BF16)),
            tokens_first(cot, mm("td,rd->tr", cot, out_right).astype(BF16)),
        ],
        0,
    )
    got_bwd = to_row(bwd)
    fwd_y = (to_y(fwd, 1), to_y(fwd, -1), to_y(fwd, 2))
    got_w, got_bwd = together(got_w, got_bwd)

    w0 = jnp.concatenate([mine_w, got_w], 2)
    bwd = all_channels(bwd, got_bwd)
    plus1, minus1 = to_z(w0, 1), to_z(w0, -1)
    pair_bwd = to_pair(bwd)
    pair_bwd, *fwd_y = together(pair_bwd, *fwd_y)
    bwd = jnp.stack([bwd, pair_bwd])
    bwd_y = (to_y(bwd, 1), to_y(bwd, -1), to_y(bwd, 2))
    plus1, minus1, sent_bwd = together(plus1, minus1, bwd)

    plus2, minus2 = to_z(plus1, 1), to_z(minus1, -1)
    fwd = jnp.stack([fwd, *fwd_y])
    got_fwd = to_row(fwd)
    right_own, right_other = own_units(pair, z, row, up_right[0].T)
    left_own, left_other = own_units(pair, z, row, down_left[0])
    plus2, minus2, got_fwd = together(plus2, minus2, got_fwd)

    plus3, minus3 = to_z(plus2, 1), to_z(minus2, -1)
    fwd = all_channels(fwd, got_fwd)
    pair_fwd = to_pair(fwd)
    got_units = to_pair(jnp.stack([right_other, left_other]))
    plus3, minus3, pair_fwd, got_units, *bwd_y = together(plus3, minus3, pair_fwd, got_units, *bwd_y)

    bwd = jnp.stack([bwd, *bwd_y], 1)
    core_bwd = to_core(bwd)
    far_up, far_down = to_z(plus3[0], 1), to_z(minus3[1], -1)
    fwd = jnp.stack([fwd, pair_fwd])
    core_fwd = to_core(fwd)
    far_up, far_down, core_bwd = together(far_up, far_down, core_bwd)
    in_right = jnp.stack([right_own, got_units[0]])
    out_left = jnp.stack([left_own, got_units[1]])
    up = jnp.concatenate([far_up, plus3[0], plus2[0], plus1[0], w0[0], minus1[0], minus2[0], minus3[0]], 0)
    down = jnp.concatenate([far_down, plus3[1], plus2[1], plus1[1], w0[1], minus1[1], minus2[1], minus3[1]], 0)
    bwd = jnp.stack([bwd, core_bwd], 1)
    x_bwd, cots = bwd[:, :, :, :32].reshape(2, 256, 2816), bwd[:, :, :, 32:].reshape(2, 256, 2816)
    x_fwd = jnp.stack([fwd, core_fwd], 1).reshape(2, 256, 2816)
    x_bwd, din_bwd = x_bwd[:, :, :2560], x_bwd[:, :, 2560:]
    cots, gdout = cots[:, :, :2560], cots[:, :, 2560:]
    x_fwd, din_fwd = x_fwd[:, :, :2560], x_fwd[:, :, 2560:]

    pre_bwd = mm("fd,std->fst", up, x_bwd) + mm("sfr,str->fst", in_right, din_bwd)
    sigma = jax.nn.sigmoid(pre_bwd)
    hid_bwd = (pre_bwd * sigma).astype(BF16)
    slope = sigma * (1.0 + pre_bwd * (1.0 - sigma))
    grad_hid = mm("fd,std->fst", down, cots) + mm("sfr,str->fst", out_left, gdout)
    grad_pre = (grad_hid * slope).astype(BF16)
    gdown = mm("fst,std->fd", hid_bwd, cots).astype(BF16).reshape(8, 64, 2560)
    gup = mm("fst,std->fd", grad_pre, x_bwd).astype(BF16).reshape(8, 64, 2560)

    far_up, far_down = to_z(gup[0], 1), to_z(gdown[0], -1)
    low = jnp.concatenate(
        [mm("fst,sfr->str", hid_bwd, out_left), mm("fst,sfr->str", grad_pre, in_right)], 2
    )
    low = low.astype(BF16).reshape(2, 2, 4, 32, 512)
    core_low = to_core(low[:, 1])
    units = jnp.stack([hid_bwd, grad_pre])
    pair_units = to_pair(units[:, :, 1])
    core_low, gup, gdown, grad_pre, x_fwd, din_fwd = together(core_low, gup, gdown, grad_pre, x_fwd, din_fwd)
    send_n = mm("fst,fd->std", grad_pre, up).astype(BF16).reshape(2, 2, 4, 32, 2560)
    core_n = to_core(send_n[:, 1])
    pre_fwd = mm("fd,std->fst", up, x_fwd) + mm("sfr,str->fst", in_right, din_fwd)
    hid_fwd = jax.nn.silu(pre_fwd).astype(BF16)
    send_f = jnp.concatenate(
        [mm("fst,fd->std", hid_fwd, down), mm("fst,sfr->str", hid_fwd, out_left)], 2
    )
    send_f = send_f.astype(BF16).reshape(2, 2, 4, 32, 2816)
    far_up, far_down, core_n, send_f = together(far_up, far_down, core_n, send_f)

    plus = to_z(jnp.stack([add(far_up, gup[7]).astype(BF16), gdown[7]]), 1)
    minus = to_z(jnp.stack([gup[1], add(far_down, gdown[1]).astype(BF16)]), -1)
    sum_n = jnp.concatenate(
        [add(send_n[:, 0], core_n).astype(BF16), add(low[:, 0], core_low).astype(BF16)], 3
    )
    total_n, sent_n = scatter_y(jnp.moveaxis(sum_n, 1, 0))
    core_f = to_core(send_f[:, 1])
    half_units = jnp.stack([units[:, :, 0], pair_units], 1)
    other_units = to_row(half_units)
    plus, minus, core_f, *sent_n = together(plus, minus, core_f, *sent_n)

    plus = to_z(jnp.stack([add(plus[0], gup[6]), add(plus[1], gdown[6])]).astype(BF16), 1)
    minus = to_z(jnp.stack([add(minus[0], gup[2]), add(minus[1], gdown[2])]).astype(BF16), -1)
    sum_n = total_n(*sent_n)
    pair_n = to_pair(sum_n[1])
    total_f, sent_f = scatter_y(jnp.moveaxis(add(send_f[:, 0], core_f).astype(BF16), 1, 0))
    plus, minus, pair_n, other_units, *sent_f = together(plus, minus, pair_n, other_units, *sent_f)

    plus = to_z(jnp.stack([add(plus[0], gup[5]), add(plus[1], gdown[5])]).astype(BF16), 1)
    minus = to_z(jnp.stack([add(minus[0], gup[3]), add(minus[1], gdown[3])]).astype(BF16), -1)
    sum_n = add(sum_n[0], pair_n).astype(BF16)
    row_n = to_row(sum_n[:, 1280:])
    sum_f = total_f(*sent_f)
    pair_f = to_pair(sum_f[1])
    hid_all = in_order(pair, z, row, half_units[0], other_units[0])
    pre_all = in_order(pair, z, row, half_units[1], other_units[1])
    grad_down_left = mm("ft,tr->fr", hid_all, gdout[0])
    grad_up_right = mm("tr,ft->rf", din_bwd[0], pre_all)
    plus, minus, row_n, pair_f, grad_down_left, grad_up_right = together(
        plus, minus, row_n, pair_f, grad_down_left, grad_up_right
    )

    total = add(jnp.stack([gup[4], gdown[4]]), plus, minus).astype(BF16)
    got = to_row(total[:, :, 1280:])
    sum_f = add(sum_f[0], pair_f).astype(BF16)
    row_f = to_row(sum_f[:, 1280:])
    rest = add(sum_n[:, 2560:], row_n[:, 1280:]).astype(BF16)
    rest = (rest, to_y(rest, 1), to_y(rest, -1), to_y(rest, 2))
    grad_in = add(cot, sum_n[:, :1280], row_n[:, :1280]) + mm("tr,dr->td", rest[0][:, 256:], in_left)
    handoff_bwd = to_section(grad_in.astype(BF16), -1)
    row_f, *rest = together(row_f, *rest)
    dout_own = add(sum_f[:, 2560:], row_f[:, 1280:]).astype(BF16)
    out_fwd = add(in_fwd, sum_f[:, :1280], row_f[:, :1280]) + mm("tr,rd->td", dout_own, out_right)
    handoff_fwd = to_section(out_fwd.astype(BF16), 1)
    rest = jnp.stack(rest)
    rest = jnp.concatenate([rest, to_core(rest)], 0).reshape(256, 512)
    grad_down_right = mm("tr,td->rd", rest[:, :256], cots[0, :, :1280])
    grad_up_left = mm("td,tr->dr", x_bwd[0, :, :1280], rest[:, 256:])
    return (
        handoff_fwd[None],
        handoff_bwd[None],
        from_row(row, total[0, :, :1280], got[0]).T,
        from_row(row, total[1, :, :1280], got[1]),
        grad_up_left[None],
        grad_up_right[None],
        grad_down_left[None],
        grad_down_right[None],
    )


def solution(mesh):
    in_specs = (
        P("section", "col", "row"),
        P("section", "col", "row"),
        P("section", "col", "row"),
        P("row", ("col", "section")),
        P(("col", "section"), "row"),
        P("section", "row", None),
        P("section", None, "col"),
        P("section", "col", None),
        P("section", None, "row"),
    )
    out_specs = (
        P("section", "col", "row"),
        P("section", "col", "row"),
        P("row", ("col", "section")),
        P(("col", "section"), "row"),
        P("section", "row", None),
        P("section", None, "col"),
        P("section", "col", None),
        P("section", None, "row"),
    )
    return jax.shard_map(local, mesh=mesh, in_specs=in_specs, out_specs=out_specs, check_vma=False)
```

```python
import jax
import jax.numpy as jnp
import numpy as np
from jax import lax
from jax.sharding import PartitionSpec as P

F32 = jnp.float32
BF16 = jnp.bfloat16
PLACE = (2, 8, 2, 4, 2)
AXES = ("section", "row", "col")
Z_GROUPS = [list(range(8)), list(range(8, 16))]


def send(block, move):
    route = []
    for src in np.ndindex(*PLACE):
        dst = tuple(int(d) % n for d, n in zip(move(*src), PLACE))
        route.append((int(np.ravel_multi_index(src, PLACE)), int(np.ravel_multi_index(dst, PLACE))))
    return lax.ppermute(block, AXES, route)


def to_pair(block):
    return send(block, lambda a, z, r, y, k: (a + 1, z, r, y, k))


def to_row(block):
    return send(block, lambda a, z, r, y, k: (a, z, r + 1, y, k))


def to_core(block):
    return send(block, lambda a, z, r, y, k: (a, z, r, y, k + 1))


def to_y(block, hop):
    return send(block, lambda a, z, r, y, k: (a, z, r, y + hop, k))


def to_section(block, hop):
    def move(a, z, r, y, k):
        s = (a * 8 + z + hop) % 16
        return (s // 8, s % 8, r, y, k)

    return send(block, move)


def pick(block, index, axis):
    return lax.dynamic_index_in_dim(block, index, axis, keepdims=False)


def mm(subscripts, left, right):
    return jnp.einsum(subscripts, left, right, preferred_element_type=F32)


def add(*terms):
    total = terms[0].astype(F32)
    for term in terms[1:]:
        total = total + term.astype(F32)
    return total


def together(*blocks):
    return lax.optimization_barrier(blocks)


def tokens_first(block, part):
    return jnp.concatenate([block, part], -1)


def all_channels(mine, other):
    return jnp.concatenate(
        [mine[..., :1280], other[..., :1280], add(mine[..., 1280:], other[..., 1280:]).astype(BF16)], -1
    )


def scatter_y(block):
    sent = (to_y(block[1], -1), to_y(block[2], 1), to_y(block[3], 2))
    return lambda *got: add(block[0], *got).astype(BF16), sent


def from_row(row, mine, other):
    first = jnp.where(row == 0, mine, other)
    second = jnp.where(row == 0, other, mine)
    return jnp.concatenate([first, second], 0)


def in_order(pair, row, half, other):
    whole = jnp.stack([half, other]).reshape(2, 2, 8, 64, 256)
    whole = jnp.where(row == 0, whole, whole[::-1])
    whole = jnp.where(pair == 0, whole, whole[:, ::-1])
    return jnp.transpose(whole, (1, 2, 0, 3, 4)).reshape(2048, 256)


def own_units(pair, row, factor):
    units = pick(factor.reshape(2, 8, 2, 64, 256), row, 2)
    mine, other = pick(units, pair, 0), pick(units, 1 - pair, 0)
    return mine.reshape(512, 256), other.reshape(512, 256)


def local(
    input_fwd,
    input_bwd,
    cotangent,
    shared_up,
    shared_down,
    up_left,
    up_right,
    down_left,
    down_right,
):
    section, row = lax.axis_index("section"), lax.axis_index("row")
    pair = section // 8
    in_fwd, in_bwd, cot = input_fwd[0], input_bwd[0], cotangent[0]
    in_left, out_right = up_left[0], down_right[0]

    halves = jnp.stack([shared_up.T, shared_down]).reshape(2, 2, 64, 1280)
    mine_w = pick(halves, row, 1)
    give_w = pick(halves, 1 - row, 1)
    got_w = to_row(give_w)
    give_w, in_fwd, in_bwd, cot = together(give_w, in_fwd, in_bwd, cot)

    fwd = tokens_first(in_fwd, mm("td,dr->tr", in_fwd, in_left).astype(BF16))
    bwd = jnp.concatenate(
        [
            tokens_first(in_bwd, mm("td,dr->tr", in_bwd, in_left).astype(BF16)),
            tokens_first(cot, mm("td,rd->tr", cot, out_right).astype(BF16)),
        ],
        0,
    )
    got_bwd = to_row(bwd)
    fwd_y = (to_y(fwd, 1), to_y(fwd, -1), to_y(fwd, 2))
    got_w, got_bwd = together(got_w, got_bwd)

    weights = lax.all_gather(
        jnp.concatenate([mine_w, got_w], 2), "section", axis=1, tiled=True, axis_index_groups=Z_GROUPS
    )
    bwd = all_channels(bwd, got_bwd)
    bwd = jnp.stack([bwd, to_pair(bwd)])
    bwd = jnp.stack([bwd, to_y(bwd, 1), to_y(bwd, -1), to_y(bwd, 2)], 1)
    core_bwd = to_core(bwd)
    fwd = jnp.stack([fwd, *fwd_y])
    fwd = all_channels(fwd, to_row(fwd))
    fwd = jnp.stack([fwd, to_pair(fwd)])
    right_own, right_other = own_units(pair, row, up_right[0].T)
    left_own, left_other = own_units(pair, row, down_left[0])
    got_units = to_pair(jnp.stack([right_other, left_other]))
    core_fwd = to_core(fwd)
    weights, core_bwd, core_fwd, got_units = together(weights, core_bwd, core_fwd, got_units)
    up, down = weights[0], weights[1]
    in_right = jnp.stack([right_own, got_units[0]])
    out_left = jnp.stack([left_own, got_units[1]])
    bwd = jnp.stack([bwd, core_bwd], 1)
    x_bwd, cots = bwd[:, :, :, :32].reshape(2, 256, 2816), bwd[:, :, :, 32:].reshape(2, 256, 2816)
    x_fwd = jnp.stack([fwd, core_fwd], 1).reshape(2, 256, 2816)
    x_bwd, din_bwd = x_bwd[:, :, :2560], x_bwd[:, :, 2560:]
    cots, gdout = cots[:, :, :2560], cots[:, :, 2560:]
    x_fwd, din_fwd = x_fwd[:, :, :2560], x_fwd[:, :, 2560:]

    pre_bwd = mm("fd,std->fst", up, x_bwd) + mm("sfr,str->fst", in_right, din_bwd)
    sigma = jax.nn.sigmoid(pre_bwd)
    hid_bwd = (pre_bwd * sigma).astype(BF16)
    slope = sigma * (1.0 + pre_bwd * (1.0 - sigma))
    grad_hid = mm("fd,std->fst", down, cots) + mm("sfr,str->fst", out_left, gdout)
    grad_pre = (grad_hid * slope).astype(BF16)
    grads = jnp.stack(
        [mm("fst,std->fd", grad_pre, x_bwd).astype(BF16), mm("fst,std->fd", hid_bwd, cots).astype(BF16)]
    )
    total = lax.psum_scatter(
        grads, "section", scatter_dimension=1, tiled=True, axis_index_groups=Z_GROUPS
    )
    low = jnp.concatenate(
        [mm("fst,sfr->str", hid_bwd, out_left), mm("fst,sfr->str", grad_pre, in_right)], 2
    )
    low = low.astype(BF16).reshape(2, 2, 4, 32, 512)
    core_low = to_core(low[:, 1])
    units = jnp.stack([hid_bwd, grad_pre])
    pair_units = to_pair(units[:, :, 1])
    core_low, grads, grad_pre, x_fwd, din_fwd = together(core_low, grads, grad_pre, x_fwd, din_fwd)
    send_n = mm("fst,fd->std", grad_pre, up).astype(BF16).reshape(2, 2, 4, 32, 2560)
    core_n = to_core(send_n[:, 1])
    pre_fwd = mm("fd,std->fst", up, x_fwd) + mm("sfr,str->fst", in_right, din_fwd)
    hid_fwd = jax.nn.silu(pre_fwd).astype(BF16)
    send_f = jnp.concatenate(
        [mm("fst,fd->std", hid_fwd, down), mm("fst,sfr->str", hid_fwd, out_left)], 2
    )
    send_f = send_f.astype(BF16).reshape(2, 2, 4, 32, 2816)
    sum_n = jnp.concatenate(
        [add(send_n[:, 0], core_n).astype(BF16), add(low[:, 0], core_low).astype(BF16)], 3
    )
    total_n, sent_n = scatter_y(jnp.moveaxis(sum_n, 1, 0))
    core_f = to_core(send_f[:, 1])
    half_units = jnp.stack([units[:, :, 0], pair_units], 1)
    other_units = to_row(half_units)
    sum_n = total_n(*sent_n)
    sum_n = add(sum_n[0], to_pair(sum_n[1])).astype(BF16)
    row_n = to_row(sum_n[:, 1280:])
    total_f, sent_f = scatter_y(jnp.moveaxis(add(send_f[:, 0], core_f).astype(BF16), 1, 0))
    other_units, *sent_f = together(other_units, *sent_f)
    sum_f = total_f(*sent_f)
    sum_f = add(sum_f[0], to_pair(sum_f[1])).astype(BF16)
    row_f = to_row(sum_f[:, 1280:])
    rest = add(sum_n[:, 2560:], row_n[:, 1280:]).astype(BF16)
    grad_in = add(cot, sum_n[:, :1280], row_n[:, :1280]) + mm("tr,dr->td", rest[:, 256:], in_left)
    handoff_bwd = to_section(grad_in.astype(BF16), -1)
    rest = jnp.stack([rest, to_y(rest, 1), to_y(rest, -1), to_y(rest, 2)])
    rest = jnp.concatenate([rest, to_core(rest)], 0).reshape(256, 512)
    dout_own = add(sum_f[:, 2560:], row_f[:, 1280:]).astype(BF16)
    out_fwd = add(in_fwd, sum_f[:, :1280], row_f[:, :1280]) + mm("tr,rd->td", dout_own, out_right)
    handoff_fwd = to_section(out_fwd.astype(BF16), 1)
    grad_down_right = mm("tr,td->rd", rest[:, :256], cots[0, :, :1280])
    grad_up_left = mm("td,tr->dr", x_bwd[0, :, :1280], rest[:, 256:])
    hid_all = in_order(pair, row, half_units[0], other_units[0])
    pre_all = in_order(pair, row, half_units[1], other_units[1])
    grad_down_left = mm("ft,tr->fr", hid_all, gdout[0])
    grad_up_right = mm("tr,ft->rf", din_bwd[0], pre_all)
    total, grad_down_right, grad_up_left, grad_down_left, grad_up_right, handoff_fwd, handoff_bwd = together(
        total, grad_down_right, grad_up_left, grad_down_left, grad_up_right, handoff_fwd, handoff_bwd
    )
    got = to_row(total[:, :, 1280:])
    return (
        handoff_fwd[None],
        handoff_bwd[None],
        from_row(row, total[0, :, :1280], got[0]).T,
        from_row(row, total[1, :, :1280], got[1]),
        grad_up_left[None],
        grad_up_right[None],
        grad_down_left[None],
        grad_down_right[None],
    )


def solution(mesh):
    in_specs = (
        P("section", "col", "row"),
        P("section", "col", "row"),
        P("section", "col", "row"),
        P("row", ("col", "section")),
        P(("col", "section"), "row"),
        P("section", "row", None),
        P("section", None, "col"),
        P("section", "col", None),
        P("section", None, "row"),
    )
    out_specs = (
        P("section", "col", "row"),
        P("section", "col", "row"),
        P("row", ("col", "section")),
        P(("col", "section"), "row"),
        P("section", "row", None),
        P("section", None, "col"),
        P("section", "col", None),
        P("section", None, "row"),
    )
    return jax.shard_map(local, mesh=mesh, in_specs=in_specs, out_specs=out_specs, check_vma=False)
```

```python
import jax
import jax.numpy as jnp
import numpy as np
from jax import lax
from jax.sharding import PartitionSpec as P

F32 = jnp.float32
BF16 = jnp.bfloat16
PLACE = (2, 8, 2, 4, 2)
AXES = ("section", "row", "col")
Z_GROUPS = [list(range(8)), list(range(8, 16))]


def send(block, move):
    route = []
    for src in np.ndindex(*PLACE):
        dst = tuple(int(d) % n for d, n in zip(move(*src), PLACE))
        route.append((int(np.ravel_multi_index(src, PLACE)), int(np.ravel_multi_index(dst, PLACE))))
    return lax.ppermute(block, AXES, route)


def to_pair(block):
    return send(block, lambda a, z, r, y, k: (a + 1, z, r, y, k))


def to_row(block):
    return send(block, lambda a, z, r, y, k: (a, z, r + 1, y, k))


def to_core(block):
    return send(block, lambda a, z, r, y, k: (a, z, r, y, k + 1))


def to_y(block, hop):
    return send(block, lambda a, z, r, y, k: (a, z, r, y + hop, k))


def to_section(block, hop):
    def move(a, z, r, y, k):
        s = (a * 8 + z + hop) % 16
        return (s // 8, s % 8, r, y, k)

    return send(block, move)


def pick(block, index, axis):
    return lax.dynamic_index_in_dim(block, index, axis, keepdims=False)


def mm(subscripts, left, right):
    return jnp.einsum(subscripts, left, right, preferred_element_type=F32)


def add(*terms):
    total = terms[0].astype(F32)
    for term in terms[1:]:
        total = total + term.astype(F32)
    return total


def together(*blocks):
    return lax.optimization_barrier(blocks)


def tokens_first(block, part):
    return jnp.concatenate([block, part], -1)


def all_channels(mine, other):
    return jnp.concatenate(
        [mine[..., :1280], other[..., :1280], add(mine[..., 1280:], other[..., 1280:]).astype(BF16)], -1
    )


def scatter_y(block):
    sent = (to_y(block[1], -1), to_y(block[2], 1), to_y(block[3], 2))
    return lambda *got: add(block[0], *got).astype(BF16), sent


def from_row(row, mine, other):
    first = jnp.where(row == 0, mine, other)
    second = jnp.where(row == 0, other, mine)
    return jnp.concatenate([first, second], 0)


def in_order(pair, row, half, other):
    whole = jnp.stack([half, other]).reshape(2, 2, 8, 64, 256)
    whole = jnp.where(row == 0, whole, whole[::-1])
    whole = jnp.where(pair == 0, whole, whole[:, ::-1])
    return jnp.transpose(whole, (1, 2, 0, 3, 4)).reshape(2048, 256)


def own_units(pair, row, factor):
    units = pick(factor.reshape(2, 8, 2, 64, 256), row, 2)
    mine, other = pick(units, pair, 0), pick(units, 1 - pair, 0)
    return mine.reshape(512, 256), other.reshape(512, 256)


def local(
    input_fwd,
    input_bwd,
    cotangent,
    shared_up,
    shared_down,
    up_left,
    up_right,
    down_left,
    down_right,
):
    section, row = lax.axis_index("section"), lax.axis_index("row")
    pair = section // 8
    in_fwd, in_bwd, cot = input_fwd[0], input_bwd[0], cotangent[0]
    in_left, out_right = up_left[0], down_right[0]

    halves = jnp.stack([shared_up.T, shared_down]).reshape(2, 2, 64, 1280)
    mine_w = pick(halves, row, 1)
    give_w = pick(halves, 1 - row, 1)
    got_w = to_row(give_w)
    give_w, in_fwd, in_bwd, cot = together(give_w, in_fwd, in_bwd, cot)

    fwd = tokens_first(in_fwd, mm("td,dr->tr", in_fwd, in_left).astype(BF16))
    bwd = jnp.concatenate(
        [
            tokens_first(in_bwd, mm("td,dr->tr", in_bwd, in_left).astype(BF16)),
            tokens_first(cot, mm("td,rd->tr", cot, out_right).astype(BF16)),
        ],
        0,
    )
    got_w, bwd, fwd = together(got_w, bwd, fwd)

    weights = lax.all_gather(
        jnp.concatenate([mine_w, got_w], 2), "section", axis=1, tiled=True, axis_index_groups=Z_GROUPS
    )
    got_bwd = to_row(bwd)
    fwd_y = (to_y(fwd, 1), to_y(fwd, -1), to_y(fwd, 2))
    right_own, right_other = own_units(pair, row, up_right[0].T)
    left_own, left_other = own_units(pair, row, down_left[0])
    got_bwd, right_other, left_other, *fwd_y = together(got_bwd, right_other, left_other, *fwd_y)
    bwd = all_channels(bwd, got_bwd)
    pair_bwd = to_pair(bwd)
    got_units = to_pair(jnp.stack([right_other, left_other]))
    fwd = jnp.stack([fwd, *fwd_y])
    got_fwd = to_row(fwd)
    bwd = jnp.stack([bwd, pair_bwd])
    bwd_y = (to_y(bwd, 1), to_y(bwd, -1), to_y(bwd, 2))
    got_fwd, got_units, bwd = together(got_fwd, got_units, bwd)
    fwd = all_channels(fwd, got_fwd)
    pair_fwd = to_pair(fwd)
    bwd = jnp.stack([bwd, *bwd_y], 1).reshape(2, 4, 2, 32, 2816)
    core_bwd = to_core(bwd)
    weights, core_bwd = together(weights, core_bwd)
    fwd = jnp.stack([fwd, pair_fwd])
    core_fwd = to_core(fwd)
    up, down = weights[0], weights[1]
    in_right = jnp.stack([right_own, got_units[0]])
    out_left = jnp.stack([left_own, got_units[1]])
    bwd = jnp.transpose(jnp.stack([bwd, core_bwd], 1), (3, 0, 1, 2, 4, 5)).reshape(2, 2, 256, 2816)
    x_bwd, din_bwd = bwd[0, :, :, :2560], bwd[0, :, :, 2560:]
    cots, gdout = bwd[1, :, :, :2560], bwd[1, :, :, 2560:]

    pre_bwd = mm("fd,std->fst", up, x_bwd) + mm("sfr,str->fst", in_right, din_bwd)
    sigma = jax.nn.sigmoid(pre_bwd)
    hid_bwd = (pre_bwd * sigma).astype(BF16)
    slope = sigma * (1.0 + pre_bwd * (1.0 - sigma))
    grad_hid = mm("fd,std->fst", down, cots) + mm("sfr,str->fst", out_left, gdout)
    grad_pre = (grad_hid * slope).astype(BF16)
    units = jnp.stack([grad_pre, hid_bwd])
    grads = mm("ufst,ustd->ufd", units, bwd[:, :, :, :2560]).astype(BF16)
    total = lax.psum_scatter(
        grads, "section", scatter_dimension=1, tiled=True, axis_index_groups=Z_GROUPS
    )
    grads, units, grad_pre, hid_bwd = together(grads, units, grad_pre, hid_bwd)
    pair_units = to_pair(units[:, :, 1])
    low = jnp.concatenate(
        [mm("fst,sfr->str", hid_bwd, out_left), mm("fst,sfr->str", grad_pre, in_right)], 2
    )
    low = low.astype(BF16).reshape(2, 2, 4, 32, 512)
    core_low = to_core(low[:, 1])
    send_n = mm("fst,fd->std", grad_pre, up).astype(BF16).reshape(2, 2, 4, 32, 2560)
    core_n = to_core(send_n[:, 1])
    core_n, core_low, fwd, core_fwd = together(core_n, core_low, fwd, core_fwd)
    x_fwd = jnp.stack([fwd, core_fwd], 1).reshape(2, 256, 2816)
    x_fwd, din_fwd = x_fwd[:, :, :2560], x_fwd[:, :, 2560:]
    pre_fwd = mm("fd,std->fst", up, x_fwd) + mm("sfr,str->fst", in_right, din_fwd)
    hid_fwd = jax.nn.silu(pre_fwd).astype(BF16)
    send_f = jnp.concatenate(
        [mm("fst,fd->std", hid_fwd, down), mm("fst,sfr->str", hid_fwd, out_left)], 2
    )
    send_f = send_f.astype(BF16).reshape(2, 2, 4, 32, 2816)
    sum_n = jnp.concatenate(
        [add(send_n[:, 0], core_n).astype(BF16), add(low[:, 0], core_low).astype(BF16)], 3
    )
    total_n, sent_n = scatter_y(jnp.moveaxis(sum_n, 1, 0))
    half_units = jnp.stack([units[:, :, 0], pair_units], 1)
    other_units = to_row(half_units)
    core_f = to_core(send_f[:, 1])
    core_f, *sent_n = together(core_f, *sent_n)
    sum_n = total_n(*sent_n)
    sum_n = add(sum_n[0], to_pair(sum_n[1])).astype(BF16)
    row_n = to_row(sum_n[:, 1280:])
    total_f, sent_f = scatter_y(jnp.moveaxis(add(send_f[:, 0], core_f).astype(BF16), 1, 0))
    other_units, *sent_f = together(other_units, *sent_f)
    sum_f = total_f(*sent_f)
    sum_f = add(sum_f[0], to_pair(sum_f[1])).astype(BF16)
    row_f = to_row(sum_f[:, 1280:])
    rest = add(sum_n[:, 2560:], row_n[:, 1280:]).astype(BF16)
    grad_in = add(cot, sum_n[:, :1280], row_n[:, :1280]) + mm("tr,dr->td", rest[:, 256:], in_left)
    handoff_bwd = to_section(grad_in.astype(BF16), -1)
    rest = jnp.stack([rest, to_y(rest, 1), to_y(rest, -1), to_y(rest, 2)])
    core_rest = to_core(rest)
    hid_all = in_order(pair, row, half_units[1], other_units[1])
    pre_all = in_order(pair, row, half_units[0], other_units[0])
    grad_down_left = mm("ft,tr->fr", hid_all, gdout[0])
    grad_up_right = mm("tr,ft->rf", din_bwd[0], pre_all)
    total, row_f, core_rest, handoff_bwd, grad_down_left, grad_up_right = together(
        total, row_f, core_rest, handoff_bwd, grad_down_left, grad_up_right
    )
    got = to_row(total[:, :, 1280:])
    dout_own = add(sum_f[:, 2560:], row_f[:, 1280:]).astype(BF16)
    out_fwd = add(in_fwd, sum_f[:, :1280], row_f[:, :1280]) + mm("tr,rd->td", dout_own, out_right)
    handoff_fwd = to_section(out_fwd.astype(BF16), 1)
    rest = jnp.concatenate([rest, core_rest], 0).reshape(256, 512)
    grad_down_right = mm("tr,td->rd", rest[:, :256], cots[0, :, :1280])
    grad_up_left = mm("td,tr->dr", x_bwd[0, :, :1280], rest[:, 256:])
    return (
        handoff_fwd[None],
        handoff_bwd[None],
        from_row(row, total[0, :, :1280], got[0]).T,
        from_row(row, total[1, :, :1280], got[1]),
        grad_up_left[None],
        grad_up_right[None],
        grad_down_left[None],
        grad_down_right[None],
    )


def solution(mesh):
    in_specs = (
        P("section", "col", "row"),
        P("section", "col", "row"),
        P("section", "col", "row"),
        P("row", ("col", "section")),
        P(("col", "section"), "row"),
        P("section", "row", None),
        P("section", None, "col"),
        P("section", "col", None),
        P("section", None, "row"),
    )
    out_specs = (
        P("section", "col", "row"),
        P("section", "col", "row"),
        P("row", ("col", "section")),
        P(("col", "section"), "row"),
        P("section", "row", None),
        P("section", None, "col"),
        P("section", "col", None),
        P("section", None, "row"),
    )
    return jax.shard_map(local, mesh=mesh, in_specs=in_specs, out_specs=out_specs, check_vma=False)
```

```python
import jax
import jax.numpy as jnp
import numpy as np
from jax import lax
from jax.sharding import PartitionSpec as P

F32 = jnp.float32
BF16 = jnp.bfloat16
PLACE = (2, 8, 2, 4, 2)
AXES = ("section", "row", "col")
Z_GROUPS = [list(range(8)), list(range(8, 16))]


def send(block, move):
    route = []
    for src in np.ndindex(*PLACE):
        dst = tuple(int(d) % n for d, n in zip(move(*src), PLACE))
        route.append((int(np.ravel_multi_index(src, PLACE)), int(np.ravel_multi_index(dst, PLACE))))
    return lax.ppermute(block, AXES, route)


def to_pair(block):
    return send(block, lambda a, z, r, y, k: (a + 1, z, r, y, k))


def to_row(block):
    return send(block, lambda a, z, r, y, k: (a, z, r + 1, y, k))


def to_core(block):
    return send(block, lambda a, z, r, y, k: (a, z, r, y, k + 1))


def to_y(block, hop):
    return send(block, lambda a, z, r, y, k: (a, z, r, y + hop, k))


def to_section(block, hop):
    def move(a, z, r, y, k):
        s = (a * 8 + z + hop) % 16
        return (s // 8, s % 8, r, y, k)

    return send(block, move)


def pick(block, index, axis):
    return lax.dynamic_index_in_dim(block, index, axis, keepdims=False)


def mm(subscripts, left, right):
    return jnp.einsum(subscripts, left, right, preferred_element_type=F32)


def add(*terms):
    total = terms[0].astype(F32)
    for term in terms[1:]:
        total = total + term.astype(F32)
    return total


def together(*blocks):
    return lax.optimization_barrier(blocks)


def tokens_first(block, part):
    return jnp.concatenate([block, part], -1)


def all_channels(mine, other):
    return jnp.concatenate(
        [mine[..., :1280], other[..., :1280], add(mine[..., 1280:], other[..., 1280:]).astype(BF16)], -1
    )


def scatter_y(block):
    sent = (to_y(block[1], -1), to_y(block[2], 1), to_y(block[3], 2))
    return lambda *got: add(block[0], *got).astype(BF16), sent


def from_row(row, mine, other):
    first = jnp.where(row == 0, mine, other)
    second = jnp.where(row == 0, other, mine)
    return jnp.concatenate([first, second], 0)


def in_order(pair, row, half, other):
    whole = jnp.stack([half, other]).reshape(2, 2, 8, 64, 256)
    whole = jnp.where(row == 0, whole, whole[::-1])
    whole = jnp.where(pair == 0, whole, whole[:, ::-1])
    return jnp.transpose(whole, (1, 2, 0, 3, 4)).reshape(2048, 256)


def own_units(pair, row, factor):
    units = pick(factor.reshape(2, 8, 2, 64, 256), row, 2)
    mine, other = pick(units, pair, 0), pick(units, 1 - pair, 0)
    return mine.reshape(512, 256), other.reshape(512, 256)


def local(
    input_fwd,
    input_bwd,
    cotangent,
    shared_up,
    shared_down,
    up_left,
    up_right,
    down_left,
    down_right,
):
    section, row = lax.axis_index("section"), lax.axis_index("row")
    pair = section // 8
    in_fwd, in_bwd, cot = input_fwd[0], input_bwd[0], cotangent[0]
    in_left, out_right = up_left[0], down_right[0]

    halves = jnp.stack([shared_up.T, shared_down]).reshape(2, 2, 64, 1280)
    mine_w = pick(halves, row, 1)
    give_w = pick(halves, 1 - row, 1)
    got_w = to_row(give_w)
    give_w, in_fwd, in_bwd, cot = together(give_w, in_fwd, in_bwd, cot)

    fwd = tokens_first(in_fwd, mm("td,dr->tr", in_fwd, in_left).astype(BF16))
    bwd = jnp.concatenate(
        [
            tokens_first(in_bwd, mm("td,dr->tr", in_bwd, in_left).astype(BF16)),
            tokens_first(cot, mm("td,rd->tr", cot, out_right).astype(BF16)),
        ],
        0,
    )
    got_w, bwd, fwd = together(got_w, bwd, fwd)

    weights = lax.all_gather(
        jnp.concatenate([mine_w, got_w], 2), "section", axis=1, tiled=True, axis_index_groups=Z_GROUPS
    )
    got_bwd = to_row(bwd)
    fwd_y = (to_y(fwd, 1), to_y(fwd, -1), to_y(fwd, 2))
    right_own, right_other = own_units(pair, row, up_right[0].T)
    left_own, left_other = own_units(pair, row, down_left[0])
    got_bwd, right_other, left_other, *fwd_y = together(got_bwd, right_other, left_other, *fwd_y)
    bwd = all_channels(bwd, got_bwd)
    pair_bwd = to_pair(bwd)
    got_units = to_pair(jnp.stack([right_other, left_other]))
    fwd = jnp.stack([fwd, *fwd_y])
    got_fwd = to_row(fwd)
    bwd = jnp.stack([bwd, pair_bwd])
    bwd_y = (to_y(bwd, 1), to_y(bwd, -1), to_y(bwd, 2))
    got_fwd, got_units, bwd = together(got_fwd, got_units, bwd)
    fwd = all_channels(fwd, got_fwd)
    pair_fwd = to_pair(fwd)
    bwd = jnp.stack([bwd, *bwd_y], 1).reshape(2, 4, 2, 32, 2816)
    core_bwd = to_core(bwd)
    weights, core_bwd = together(weights, core_bwd)
    up, down = weights[0], weights[1]
    in_right = jnp.stack([right_own, got_units[0]])
    out_left = jnp.stack([left_own, got_units[1]])
    bwd = jnp.transpose(jnp.stack([bwd, core_bwd], 1), (3, 0, 1, 2, 4, 5)).reshape(2, 2, 256, 2816)
    x_bwd, din_bwd = bwd[0, :, :, :2560], bwd[0, :, :, 2560:]
    cots, gdout = bwd[1, :, :, :2560], bwd[1, :, :, 2560:]

    pre_bwd = mm("fd,std->fst", up, x_bwd) + mm("sfr,str->fst", in_right, din_bwd)
    sigma = jax.nn.sigmoid(pre_bwd)
    hid_bwd = (pre_bwd * sigma).astype(BF16)
    slope = sigma * (1.0 + pre_bwd * (1.0 - sigma))
    hid_bwd, pair_fwd = together(hid_bwd, pair_fwd)
    fwd = jnp.stack([fwd, pair_fwd])
    core_fwd = to_core(fwd)
    grad_hid = mm("fd,std->fst", down, cots) + mm("sfr,str->fst", out_left, gdout)
    grad_pre = (grad_hid * slope).astype(BF16)
    units = jnp.stack([grad_pre, hid_bwd])
    grads = mm("ufst,ustd->ufd", units, bwd[:, :, :, :2560]).astype(BF16)
    total = lax.psum_scatter(
        grads, "section", scatter_dimension=1, tiled=True, axis_index_groups=Z_GROUPS
    )
    grads, units, grad_pre, hid_bwd, fwd, core_fwd = together(grads, units, grad_pre, hid_bwd, fwd, core_fwd)
    pair_units = to_pair(units[:, :, 1])
    low = jnp.concatenate(
        [mm("fst,sfr->str", hid_bwd, out_left), mm("fst,sfr->str", grad_pre, in_right)], 2
    )
    low = low.astype(BF16).reshape(2, 2, 4, 32, 512)
    core_low = to_core(low[:, 1])
    send_n = mm("fst,fd->std", grad_pre, up).astype(BF16).reshape(2, 2, 4, 32, 2560)
    core_n = to_core(send_n[:, 1])
    x_fwd = jnp.stack([fwd, core_fwd], 1).reshape(2, 256, 2816)
    x_fwd, din_fwd = x_fwd[:, :, :2560], x_fwd[:, :, 2560:]
    pre_fwd = mm("fd,std->fst", up, x_fwd) + mm("sfr,str->fst", in_right, din_fwd)
    hid_fwd = jax.nn.silu(pre_fwd).astype(BF16)
    send_f = jnp.concatenate(
        [mm("fst,fd->std", hid_fwd, down), mm("fst,sfr->str", hid_fwd, out_left)], 2
    )
    send_f = send_f.astype(BF16).reshape(2, 2, 4, 32, 2816)
    core_n, core_low, send_f, pair_units = together(core_n, core_low, send_f, pair_units)

    half_units = jnp.stack([units[:, :, 0], pair_units], 1)
    other_units = to_row(half_units)
    sum_n = jnp.concatenate(
        [add(send_n[:, 0], core_n).astype(BF16), add(low[:, 0], core_low).astype(BF16)], 3
    )
    total_n, sent_n = scatter_y(jnp.moveaxis(sum_n, 1, 0))
    core_f = to_core(send_f[:, 1])
    send_f, core_f, *sent_n = together(send_f, core_f, *sent_n)

    total_f, sent_f = scatter_y(jnp.moveaxis(add(send_f[:, 0], core_f).astype(BF16), 1, 0))
    sum_n = total_n(*sent_n)
    pair_n = to_pair(sum_n[1])
    pair_n, other_units, *sent_f = together(pair_n, other_units, *sent_f)

    sum_n = add(sum_n[0], pair_n).astype(BF16)
    row_n = to_row(sum_n[:, 1280:])
    sum_f = total_f(*sent_f)
    pair_f = to_pair(sum_f[1])
    hid_all = in_order(pair, row, half_units[1], other_units[1])
    pre_all = in_order(pair, row, half_units[0], other_units[0])
    row_n, pair_f = together(row_n, pair_f)

    sum_f = add(sum_f[0], pair_f).astype(BF16)
    row_f = to_row(sum_f[:, 1280:])
    rest = add(sum_n[:, 2560:], row_n[:, 1280:]).astype(BF16)
    grad_in = add(cot, sum_n[:, :1280], row_n[:, :1280]) + mm("tr,dr->td", rest[:, 256:], in_left)
    handoff_bwd = to_section(grad_in.astype(BF16), -1)
    rest = (rest, to_y(rest, 1), to_y(rest, -1), to_y(rest, 2))
    grad_down_left = mm("ft,tr->fr", hid_all, gdout[0])
    grad_up_right = mm("tr,ft->rf", din_bwd[0], pre_all)
    total, row_f, handoff_bwd, grad_down_left, grad_up_right, *rest = together(
        total, row_f, handoff_bwd, grad_down_left, grad_up_right, *rest
    )

    got = to_row(total[:, :, 1280:])
    rest = jnp.stack(rest)
    rest = jnp.concatenate([rest, to_core(rest)], 0).reshape(256, 512)
    dout_own = add(sum_f[:, 2560:], row_f[:, 1280:]).astype(BF16)
    out_fwd = add(in_fwd, sum_f[:, :1280], row_f[:, :1280]) + mm("tr,rd->td", dout_own, out_right)
    handoff_fwd = to_section(out_fwd.astype(BF16), 1)
    grad_down_right = mm("tr,td->rd", rest[:, :256], cots[0, :, :1280])
    grad_up_left = mm("td,tr->dr", x_bwd[0, :, :1280], rest[:, 256:])
    return (
        handoff_fwd[None],
        handoff_bwd[None],
        from_row(row, total[0, :, :1280], got[0]).T,
        from_row(row, total[1, :, :1280], got[1]),
        grad_up_left[None],
        grad_up_right[None],
        grad_down_left[None],
        grad_down_right[None],
    )


def solution(mesh):
    in_specs = (
        P("section", "col", "row"),
        P("section", "col", "row"),
        P("section", "col", "row"),
        P("row", ("col", "section")),
        P(("col", "section"), "row"),
        P("section", "row", None),
        P("section", None, "col"),
        P("section", "col", None),
        P("section", None, "row"),
    )
    out_specs = (
        P("section", "col", "row"),
        P("section", "col", "row"),
        P("row", ("col", "section")),
        P(("col", "section"), "row"),
        P("section", "row", None),
        P("section", None, "col"),
        P("section", "col", None),
        P("section", None, "row"),
    )
    return jax.shard_map(local, mesh=mesh, in_specs=in_specs, out_specs=out_specs, check_vma=False)
```

```python
import jax
import jax.numpy as jnp
import numpy as np
from jax import lax
from jax.sharding import PartitionSpec as P

F32 = jnp.float32
BF16 = jnp.bfloat16
PLACE = (2, 8, 2, 4, 2)
AXES = ("section", "row", "col")
Z_GROUPS = [list(range(8)), list(range(8, 16))]


def send(block, move):
    route = []
    for src in np.ndindex(*PLACE):
        dst = tuple(int(d) % n for d, n in zip(move(*src), PLACE))
        route.append((int(np.ravel_multi_index(src, PLACE)), int(np.ravel_multi_index(dst, PLACE))))
    return lax.ppermute(block, AXES, route)


def to_pair(block):
    return send(block, lambda a, z, r, y, k: (a + 1, z, r, y, k))


def to_row(block):
    return send(block, lambda a, z, r, y, k: (a, z, r + 1, y, k))


def to_core(block):
    return send(block, lambda a, z, r, y, k: (a, z, r, y, k + 1))


def to_y(block, hop):
    return send(block, lambda a, z, r, y, k: (a, z, r, y + hop, k))


def to_section(block, hop):
    def move(a, z, r, y, k):
        s = (a * 8 + z + hop) % 16
        return (s // 8, s % 8, r, y, k)

    return send(block, move)


def pick(block, index, axis):
    return lax.dynamic_index_in_dim(block, index, axis, keepdims=False)


def mm(subscripts, left, right):
    return jnp.einsum(subscripts, left, right, preferred_element_type=F32)


def add(*terms):
    total = terms[0].astype(F32)
    for term in terms[1:]:
        total = total + term.astype(F32)
    return total


def together(*blocks):
    return lax.optimization_barrier(blocks)


def tokens_first(block, part):
    return jnp.concatenate([block, part], -1)


def all_channels(mine, other):
    return jnp.concatenate(
        [mine[..., :1280], other[..., :1280], add(mine[..., 1280:], other[..., 1280:]).astype(BF16)], -1
    )


def scatter_y(block):
    sent = (to_y(block[1], -1), to_y(block[2], 1), to_y(block[3], 2))
    return lambda *got: add(block[0], *got).astype(BF16), sent


def from_row(row, mine, other):
    first = jnp.where(row == 0, mine, other)
    second = jnp.where(row == 0, other, mine)
    return jnp.concatenate([first, second], 0)


def in_order(pair, row, half, other):
    whole = jnp.stack([half, other]).reshape(2, 2, 8, 64, 256)
    whole = jnp.where(row == 0, whole, whole[::-1])
    whole = jnp.where(pair == 0, whole, whole[:, ::-1])
    return jnp.transpose(whole, (1, 2, 0, 3, 4)).reshape(2048, 256)


def own_units(pair, row, factor):
    units = pick(factor.reshape(2, 8, 2, 64, 256), row, 2)
    mine, other = pick(units, pair, 0), pick(units, 1 - pair, 0)
    return mine.reshape(512, 256), other.reshape(512, 256)


def local(
    input_fwd,
    input_bwd,
    cotangent,
    shared_up,
    shared_down,
    up_left,
    up_right,
    down_left,
    down_right,
):
    section, row = lax.axis_index("section"), lax.axis_index("row")
    pair = section // 8
    in_fwd, in_bwd, cot = input_fwd[0], input_bwd[0], cotangent[0]
    in_left, out_right = up_left[0], down_right[0]

    halves = jnp.stack([shared_up.T, shared_down]).reshape(2, 2, 64, 1280)
    mine_w = pick(halves, row, 1)
    give_w = pick(halves, 1 - row, 1)
    got_w = to_row(give_w)
    give_w, in_fwd, in_bwd, cot = together(give_w, in_fwd, in_bwd, cot)

    fwd = tokens_first(in_fwd, mm("td,dr->tr", in_fwd, in_left).astype(BF16))
    bwd = jnp.concatenate(
        [
            tokens_first(in_bwd, mm("td,dr->tr", in_bwd, in_left).astype(BF16)),
            tokens_first(cot, mm("td,rd->tr", cot, out_right).astype(BF16)),
        ],
        0,
    )
    got_w, bwd, fwd = together(got_w, bwd, fwd)

    weights = lax.all_gather(
        jnp.concatenate([mine_w, got_w], 2), "section", axis=1, tiled=True, axis_index_groups=Z_GROUPS
    )
    got_bwd = to_row(bwd)
    fwd_y = (to_y(fwd, 1), to_y(fwd, -1), to_y(fwd, 2))
    right_own, right_other = own_units(pair, row, up_right[0].T)
    left_own, left_other = own_units(pair, row, down_left[0])
    got_bwd, right_other, left_other, *fwd_y = together(got_bwd, right_other, left_other, *fwd_y)
    bwd = all_channels(bwd, got_bwd)
    pair_bwd = to_pair(bwd)
    got_units = to_pair(jnp.stack([right_other, left_other]))
    fwd = jnp.stack([fwd, *fwd_y])
    got_fwd = to_row(fwd)
    bwd = jnp.stack([bwd, pair_bwd])
    bwd_y = (to_y(bwd, 1), to_y(bwd, -1), to_y(bwd, 2))
    got_fwd, got_units, bwd = together(got_fwd, got_units, bwd)
    fwd = all_channels(fwd, got_fwd)
    pair_fwd = to_pair(fwd)
    bwd = jnp.stack([bwd, *bwd_y], 1).reshape(2, 4, 2, 32, 2816)
    core_bwd = to_core(bwd)
    in_right = jnp.stack([right_own, got_units[0]])
    out_left = jnp.stack([left_own, got_units[1]])
    bwd = jnp.transpose(jnp.stack([bwd, core_bwd], 1), (3, 0, 1, 2, 4, 5)).reshape(2, 2, 256, 2816)
    weights, bwd = together(weights, bwd)
    up, down = weights[0], weights[1]
    x_bwd, din_bwd = bwd[0, :, :, :2560], bwd[0, :, :, 2560:]
    cots, gdout = bwd[1, :, :, :2560], bwd[1, :, :, 2560:]

    pre_bwd = mm("fd,std->fst", up, x_bwd) + mm("sfr,str->fst", in_right, din_bwd)
    sigma = jax.nn.sigmoid(pre_bwd)
    hid_bwd = (pre_bwd * sigma).astype(BF16)
    slope = sigma * (1.0 + pre_bwd * (1.0 - sigma))
    hid_bwd, pair_fwd = together(hid_bwd, pair_fwd)
    fwd = jnp.stack([fwd, pair_fwd])
    grad_hid = mm("fd,std->fst", down, cots) + mm("sfr,str->fst", out_left, gdout)
    grad_pre = (grad_hid * slope).astype(BF16)
    units = jnp.stack([grad_pre, hid_bwd])
    grads = mm("ufst,ustd->ufd", units, bwd[:, :, :, :2560]).astype(BF16)
    total = lax.psum_scatter(
        grads, "section", scatter_dimension=1, tiled=True, axis_index_groups=Z_GROUPS
    )
    grads, units, grad_pre, hid_bwd, fwd = together(grads, units, grad_pre, hid_bwd, fwd)
    low = jnp.concatenate(
        [mm("fst,sfr->str", hid_bwd, out_left), mm("fst,sfr->str", grad_pre, in_right)], 2
    )
    low = low.astype(BF16).reshape(2, 2, 4, 32, 512)
    core_low = to_core(low[:, 1])
    send_n = mm("fst,fd->std", grad_pre, up).astype(BF16).reshape(2, 2, 4, 32, 2560)
    core_n = to_core(send_n[:, 1])
    core_n, core_low, fwd, units = together(core_n, core_low, fwd, units)
    core_fwd = to_core(fwd)
    sum_n = jnp.concatenate(
        [add(send_n[:, 0], core_n).astype(BF16), add(low[:, 0], core_low).astype(BF16)], 3
    )
    total_n, sent_n = scatter_y(jnp.moveaxis(sum_n, 1, 0))
    pair_units = to_pair(units[:, :, 1])
    x_fwd = jnp.stack([fwd, core_fwd], 1).reshape(2, 256, 2816)
    x_fwd, din_fwd = x_fwd[:, :, :2560], x_fwd[:, :, 2560:]
    pre_fwd = mm("fd,std->fst", up, x_fwd) + mm("sfr,str->fst", in_right, din_fwd)
    hid_fwd = jax.nn.silu(pre_fwd).astype(BF16)
    hid_fwd, *sent_n = together(hid_fwd, *sent_n)
    send_f = jnp.concatenate(
        [mm("fst,fd->std", hid_fwd, down), mm("fst,sfr->str", hid_fwd, out_left)], 2
    )
    send_f = send_f.astype(BF16).reshape(2, 2, 4, 32, 2816)
    pair_units, send_f = together(pair_units, send_f)
    half_units = jnp.stack([units[:, :, 0], pair_units], 1)
    other_units = to_row(half_units)
    core_f = to_core(send_f[:, 1])
    send_f, core_f = together(send_f, core_f)

    total_f, sent_f = scatter_y(jnp.moveaxis(add(send_f[:, 0], core_f).astype(BF16), 1, 0))
    sum_n = total_n(*sent_n)
    pair_n = to_pair(sum_n[1])
    pair_n, other_units, total, *sent_f = together(pair_n, other_units, total, *sent_f)

    sum_n = add(sum_n[0], pair_n).astype(BF16)
    row_n = to_row(sum_n[:, 1280:])
    sum_f = total_f(*sent_f)
    pair_f = to_pair(sum_f[1])
    hid_all = in_order(pair, row, half_units[1], other_units[1])
    pre_all = in_order(pair, row, half_units[0], other_units[0])
    got = to_row(total[:, :, 1280:])
    row_n, pair_f, got = together(row_n, pair_f, got)

    sum_f = add(sum_f[0], pair_f).astype(BF16)
    row_f = to_row(sum_f[:, 1280:])
    rest = add(sum_n[:, 2560:], row_n[:, 1280:]).astype(BF16)
    grad_in = add(cot, sum_n[:, :1280], row_n[:, :1280]) + mm("tr,dr->td", rest[:, 256:], in_left)
    handoff_bwd = to_section(grad_in.astype(BF16), -1)
    rest = (rest, to_y(rest, 1), to_y(rest, -1), to_y(rest, 2))
    grad_down_left = mm("ft,tr->fr", hid_all, gdout[0])
    grad_up_right = mm("tr,ft->rf", din_bwd[0], pre_all)
    row_f, grad_down_left, grad_up_right, *rest = together(row_f, grad_down_left, grad_up_right, *rest)

    rest = jnp.stack(rest)
    rest = jnp.concatenate([rest, to_core(rest)], 0).reshape(256, 512)
    dout_own = add(sum_f[:, 2560:], row_f[:, 1280:]).astype(BF16)
    out_fwd = add(in_fwd, sum_f[:, :1280], row_f[:, :1280]) + mm("tr,rd->td", dout_own, out_right)
    handoff_fwd = to_section(out_fwd.astype(BF16), 1)
    grad_down_right = mm("tr,td->rd", rest[:, :256], cots[0, :, :1280])
    grad_up_left = mm("td,tr->dr", x_bwd[0, :, :1280], rest[:, 256:])
    return (
        handoff_fwd[None],
        handoff_bwd[None],
        from_row(row, total[0, :, :1280], got[0]).T,
        from_row(row, total[1, :, :1280], got[1]),
        grad_up_left[None],
        grad_up_right[None],
        grad_down_left[None],
        grad_down_right[None],
    )


def solution(mesh):
    in_specs = (
        P("section", "col", "row"),
        P("section", "col", "row"),
        P("section", "col", "row"),
        P("row", ("col", "section")),
        P(("col", "section"), "row"),
        P("section", "row", None),
        P("section", None, "col"),
        P("section", "col", None),
        P("section", None, "row"),
    )
    out_specs = (
        P("section", "col", "row"),
        P("section", "col", "row"),
        P("row", ("col", "section")),
        P(("col", "section"), "row"),
        P("section", "row", None),
        P("section", None, "col"),
        P("section", "col", None),
        P("section", None, "row"),
    )
    return jax.shard_map(local, mesh=mesh, in_specs=in_specs, out_specs=out_specs, check_vma=False)
```

```python
import jax
import jax.numpy as jnp
import numpy as np
from jax import lax
from jax.sharding import PartitionSpec as P

F32 = jnp.float32
BF16 = jnp.bfloat16
PLACE = (2, 8, 2, 4, 2)
AXES = ("section", "row", "col")
Z_GROUPS = [list(range(8)), list(range(8, 16))]


def send(block, move):
    route = []
    for src in np.ndindex(*PLACE):
        dst = tuple(int(d) % n for d, n in zip(move(*src), PLACE))
        route.append((int(np.ravel_multi_index(src, PLACE)), int(np.ravel_multi_index(dst, PLACE))))
    return lax.ppermute(block, AXES, route)


def to_pair(block):
    return send(block, lambda a, z, r, y, k: (a + 1, z, r, y, k))


def to_row(block):
    return send(block, lambda a, z, r, y, k: (a, z, r + 1, y, k))


def to_core(block):
    return send(block, lambda a, z, r, y, k: (a, z, r, y, k + 1))


def to_y(block, hop):
    return send(block, lambda a, z, r, y, k: (a, z, r, y + hop, k))


def to_section(block, hop):
    def move(a, z, r, y, k):
        s = (a * 8 + z + hop) % 16
        return (s // 8, s % 8, r, y, k)

    return send(block, move)


def pick(block, index, axis):
    return lax.dynamic_index_in_dim(block, index, axis, keepdims=False)


def mm(subscripts, left, right):
    return jnp.einsum(subscripts, left, right, preferred_element_type=F32)


def add(*terms):
    total = terms[0].astype(F32)
    for term in terms[1:]:
        total = total + term.astype(F32)
    return total


def together(*blocks):
    return lax.optimization_barrier(blocks)


def tokens_first(block, part):
    return jnp.concatenate([block, part], -1)


def all_channels(mine, other):
    return jnp.concatenate(
        [mine[..., :1280], other[..., :1280], add(mine[..., 1280:], other[..., 1280:]).astype(BF16)], -1
    )


def scatter_y(block):
    sent = (to_y(block[1], -1), to_y(block[2], 1), to_y(block[3], 2))
    return lambda *got: add(block[0], *got).astype(BF16), sent


def from_row(row, mine, other):
    first = jnp.where(row == 0, mine, other)
    second = jnp.where(row == 0, other, mine)
    return jnp.concatenate([first, second], 0)


def in_order(pair, row, half, other):
    whole = jnp.stack([half, other]).reshape(2, 2, 8, 64, 256)
    whole = jnp.where(row == 0, whole, whole[::-1])
    whole = jnp.where(pair == 0, whole, whole[:, ::-1])
    return jnp.transpose(whole, (1, 2, 0, 3, 4)).reshape(2048, 256)


def own_units(pair, row, factor):
    units = pick(factor.reshape(2, 8, 2, 64, 256), row, 2)
    mine, other = pick(units, pair, 0), pick(units, 1 - pair, 0)
    return mine.reshape(512, 256), other.reshape(512, 256)


def local(
    input_fwd,
    input_bwd,
    cotangent,
    shared_up,
    shared_down,
    up_left,
    up_right,
    down_left,
    down_right,
):
    section, row = lax.axis_index("section"), lax.axis_index("row")
    pair = section // 8
    in_fwd, in_bwd, cot = input_fwd[0], input_bwd[0], cotangent[0]
    in_left, out_right = up_left[0], down_right[0]

    halves = jnp.stack([shared_up.T, shared_down]).reshape(2, 2, 64, 1280)
    mine_w = pick(halves, row, 1)
    give_w = pick(halves, 1 - row, 1)
    got_w = to_row(give_w)
    give_w, in_fwd, in_bwd, cot = together(give_w, in_fwd, in_bwd, cot)

    fwd = tokens_first(in_fwd, mm("td,dr->tr", in_fwd, in_left).astype(BF16))
    bwd = jnp.concatenate(
        [
            tokens_first(in_bwd, mm("td,dr->tr", in_bwd, in_left).astype(BF16)),
            tokens_first(cot, mm("td,rd->tr", cot, out_right).astype(BF16)),
        ],
        0,
    )
    got_w, bwd, fwd = together(got_w, bwd, fwd)

    weights = lax.all_gather(
        jnp.concatenate([mine_w, got_w], 2), "section", axis=1, tiled=True, axis_index_groups=Z_GROUPS
    )
    got_bwd = to_row(bwd)
    fwd_y = (to_y(fwd, 1), to_y(fwd, -1), to_y(fwd, 2))
    right_own, right_other = own_units(pair, row, up_right[0].T)
    left_own, left_other = own_units(pair, row, down_left[0])
    got_bwd, right_other, left_other, *fwd_y = together(got_bwd, right_other, left_other, *fwd_y)
    bwd = all_channels(bwd, got_bwd)
    pair_bwd = to_pair(bwd)
    got_units = to_pair(jnp.stack([right_other, left_other]))
    fwd = jnp.stack([fwd, *fwd_y])
    got_fwd = to_row(fwd)
    bwd = jnp.stack([bwd, pair_bwd])
    bwd_y = (to_y(bwd, 1), to_y(bwd, -1), to_y(bwd, 2))
    got_fwd, got_units, bwd = together(got_fwd, got_units, bwd)
    fwd = all_channels(fwd, got_fwd)
    pair_fwd = to_pair(fwd)
    bwd = jnp.stack([bwd, *bwd_y], 1).reshape(2, 4, 2, 32, 2816)
    core_bwd = to_core(bwd)
    in_right = jnp.stack([right_own, got_units[0]])
    out_left = jnp.stack([left_own, got_units[1]])
    bwd = jnp.transpose(jnp.stack([bwd, core_bwd], 1), (3, 0, 1, 2, 4, 5)).reshape(2, 2, 256, 2816)
    weights, bwd = together(weights, bwd)
    up, down = weights[0], weights[1]
    x_bwd, din_bwd = bwd[0, :, :, :2560], bwd[0, :, :, 2560:]
    cots, gdout = bwd[1, :, :, :2560], bwd[1, :, :, 2560:]

    pre_bwd = mm("fd,std->fst", up, x_bwd) + mm("sfr,str->fst", in_right, din_bwd)
    sigma = jax.nn.sigmoid(pre_bwd)
    hid_bwd = (pre_bwd * sigma).astype(BF16)
    slope = sigma * (1.0 + pre_bwd * (1.0 - sigma))
    hid_bwd, pair_fwd = together(hid_bwd, pair_fwd)
    fwd = jnp.stack([fwd, pair_fwd])
    grad_hid = mm("fd,std->fst", down, cots) + mm("sfr,str->fst", out_left, gdout)
    grad_pre = (grad_hid * slope).astype(BF16)
    units = jnp.stack([grad_pre, hid_bwd])
    grads = mm("ufst,ustd->ufd", units, bwd[:, :, :, :2560]).astype(BF16)
    total = lax.psum_scatter(
        grads, "section", scatter_dimension=1, tiled=True, axis_index_groups=Z_GROUPS
    )
    grads, units, grad_pre, hid_bwd, fwd = together(grads, units, grad_pre, hid_bwd, fwd)
    low = jnp.concatenate(
        [mm("fst,sfr->str", hid_bwd, out_left), mm("fst,sfr->str", grad_pre, in_right)], 2
    )
    low = low.astype(BF16).reshape(2, 2, 4, 32, 512)
    core_low = to_core(low[:, 1])
    send_n = mm("fst,fd->std", grad_pre, up).astype(BF16).reshape(2, 2, 4, 32, 2560)
    core_n = to_core(send_n[:, 1])
    core_n, core_low, fwd, units = together(core_n, core_low, fwd, units)
    core_fwd = to_core(fwd)
    sum_n = jnp.concatenate(
        [add(send_n[:, 0], core_n).astype(BF16), add(low[:, 0], core_low).astype(BF16)], 3
    )
    total_n, sent_n = scatter_y(jnp.moveaxis(sum_n, 1, 0))
    pair_units = to_pair(units[:, :, 1])
    x_fwd = jnp.stack([fwd, core_fwd], 1).reshape(2, 256, 2816)
    x_fwd, din_fwd = x_fwd[:, :, :2560], x_fwd[:, :, 2560:]
    pre_fwd = mm("fd,std->fst", up, x_fwd) + mm("sfr,str->fst", in_right, din_fwd)
    hid_fwd = jax.nn.silu(pre_fwd).astype(BF16)
    hid_fwd, pair_units, *sent_n = together(hid_fwd, pair_units, *sent_n)
    sum_n = total_n(*sent_n)
    pair_n = to_pair(sum_n[1])
    half_units = jnp.stack([units[:, :, 0], pair_units], 1)
    other_units = to_row(half_units)
    send_f = jnp.concatenate(
        [mm("fst,fd->std", hid_fwd, down), mm("fst,sfr->str", hid_fwd, out_left)], 2
    )
    send_f = send_f.astype(BF16).reshape(2, 2, 4, 32, 2816)
    core_f = to_core(send_f[:, 1])
    send_f, core_f, pair_n = together(send_f, core_f, pair_n)

    total_f, sent_f = scatter_y(jnp.moveaxis(add(send_f[:, 0], core_f).astype(BF16), 1, 0))
    sum_n = add(sum_n[0], pair_n).astype(BF16)
    row_n = to_row(sum_n[:, 1280:])
    row_n, other_units, total, *sent_f = together(row_n, other_units, total, *sent_f)

    sum_f = total_f(*sent_f)
    pair_f = to_pair(sum_f[1])
    got = to_row(total[:, :, 1280:])
    rest = add(sum_n[:, 2560:], row_n[:, 1280:]).astype(BF16)
    grad_in = add(cot, sum_n[:, :1280], row_n[:, :1280]) + mm("tr,dr->td", rest[:, 256:], in_left)
    handoff_bwd = to_section(grad_in.astype(BF16), -1)
    rest = (rest, to_y(rest, 1), to_y(rest, -1), to_y(rest, 2))
    hid_all = in_order(pair, row, half_units[1], other_units[1])
    pre_all = in_order(pair, row, half_units[0], other_units[0])
    grad_down_left = mm("ft,tr->fr", hid_all, gdout[0])
    grad_up_right = mm("tr,ft->rf", din_bwd[0], pre_all)
    pair_f, grad_down_left, grad_up_right, *rest = together(pair_f, grad_down_left, grad_up_right, *rest)

    sum_f = add(sum_f[0], pair_f).astype(BF16)
    row_f = to_row(sum_f[:, 1280:])
    rest = jnp.stack(rest)
    rest = jnp.concatenate([rest, to_core(rest)], 0).reshape(256, 512)
    grad_down_right = mm("tr,td->rd", rest[:, :256], cots[0, :, :1280])
    grad_up_left = mm("td,tr->dr", x_bwd[0, :, :1280], rest[:, 256:])
    row_f, got, grad_down_right, grad_up_left = together(row_f, got, grad_down_right, grad_up_left)
    dout_own = add(sum_f[:, 2560:], row_f[:, 1280:]).astype(BF16)
    out_fwd = add(in_fwd, sum_f[:, :1280], row_f[:, :1280]) + mm("tr,rd->td", dout_own, out_right)
    handoff_fwd = to_section(out_fwd.astype(BF16), 1)
    return (
        handoff_fwd[None],
        handoff_bwd[None],
        from_row(row, total[0, :, :1280], got[0]).T,
        from_row(row, total[1, :, :1280], got[1]),
        grad_up_left[None],
        grad_up_right[None],
        grad_down_left[None],
        grad_down_right[None],
    )


def solution(mesh):
    in_specs = (
        P("section", "col", "row"),
        P("section", "col", "row"),
        P("section", "col", "row"),
        P("row", ("col", "section")),
        P(("col", "section"), "row"),
        P("section", "row", None),
        P("section", None, "col"),
        P("section", "col", None),
        P("section", None, "row"),
    )
    out_specs = (
        P("section", "col", "row"),
        P("section", "col", "row"),
        P("row", ("col", "section")),
        P(("col", "section"), "row"),
        P("section", "row", None),
        P("section", None, "col"),
        P("section", "col", None),
        P("section", None, "row"),
    )
    return jax.shard_map(local, mesh=mesh, in_specs=in_specs, out_specs=out_specs, check_vma=False)
```

```python
import jax
import jax.numpy as jnp
import numpy as np
from jax import lax
from jax.sharding import PartitionSpec as P

F32 = jnp.float32
BF16 = jnp.bfloat16
PLACE = (2, 8, 2, 4, 2)
AXES = ("section", "row", "col")
Z_GROUPS = [list(range(8)), list(range(8, 16))]


def send(block, move):
    route = []
    for src in np.ndindex(*PLACE):
        dst = tuple(int(d) % n for d, n in zip(move(*src), PLACE))
        route.append((int(np.ravel_multi_index(src, PLACE)), int(np.ravel_multi_index(dst, PLACE))))
    return lax.ppermute(block, AXES, route)


def to_pair(block):
    return send(block, lambda a, z, r, y, k: (a + 1, z, r, y, k))


def to_row(block):
    return send(block, lambda a, z, r, y, k: (a, z, r + 1, y, k))


def to_core(block):
    return send(block, lambda a, z, r, y, k: (a, z, r, y, k + 1))


def to_y(block, hop):
    return send(block, lambda a, z, r, y, k: (a, z, r, y + hop, k))


def to_section(block, hop):
    def move(a, z, r, y, k):
        s = (a * 8 + z + hop) % 16
        return (s // 8, s % 8, r, y, k)

    return send(block, move)


def pick(block, index, axis):
    return lax.dynamic_index_in_dim(block, index, axis, keepdims=False)


def mm(subscripts, left, right):
    return jnp.einsum(subscripts, left, right, preferred_element_type=F32)


def add(*terms):
    total = terms[0].astype(F32)
    for term in terms[1:]:
        total = total + term.astype(F32)
    return total


def together(*blocks):
    return lax.optimization_barrier(blocks)


def tokens_first(block, part):
    return jnp.concatenate([block, part], -1)


def all_channels(mine, other):
    return jnp.concatenate(
        [mine[..., :1280], other[..., :1280], add(mine[..., 1280:], other[..., 1280:]).astype(BF16)], -1
    )


def scatter_y(block):
    sent = (to_y(block[1], -1), to_y(block[2], 1), to_y(block[3], 2))
    return lambda *got: add(block[0], *got).astype(BF16), sent


def from_row(row, mine, other):
    first = jnp.where(row == 0, mine, other)
    second = jnp.where(row == 0, other, mine)
    return jnp.concatenate([first, second], 0)


def in_order(pair, row, half, other):
    whole = jnp.stack([half, other]).reshape(2, 2, 8, 64, 256)
    whole = jnp.where(row == 0, whole, whole[::-1])
    whole = jnp.where(pair == 0, whole, whole[:, ::-1])
    return jnp.transpose(whole, (1, 2, 0, 3, 4)).reshape(2048, 256)


def own_units(pair, row, factor):
    units = pick(factor.reshape(2, 8, 2, 64, 256), row, 2)
    mine, other = pick(units, pair, 0), pick(units, 1 - pair, 0)
    return mine.reshape(512, 256), other.reshape(512, 256)


def local(
    input_fwd,
    input_bwd,
    cotangent,
    shared_up,
    shared_down,
    up_left,
    up_right,
    down_left,
    down_right,
):
    section, row = lax.axis_index("section"), lax.axis_index("row")
    pair = section // 8
    in_fwd, in_bwd, cot = input_fwd[0], input_bwd[0], cotangent[0]
    in_left, out_right = up_left[0], down_right[0]

    halves = jnp.stack([shared_up.T, shared_down]).reshape(2, 2, 64, 1280)
    mine_w = pick(halves, row, 1)
    give_w = pick(halves, 1 - row, 1)
    got_w = to_row(give_w)
    give_w, in_fwd, in_bwd, cot = together(give_w, in_fwd, in_bwd, cot)

    fwd = tokens_first(in_fwd, mm("td,dr->tr", in_fwd, in_left).astype(BF16))
    bwd = jnp.concatenate(
        [
            tokens_first(in_bwd, mm("td,dr->tr", in_bwd, in_left).astype(BF16)),
            tokens_first(cot, mm("td,rd->tr", cot, out_right).astype(BF16)),
        ],
        0,
    )
    got_w, bwd, fwd = together(got_w, bwd, fwd)

    weights = lax.all_gather(
        jnp.concatenate([mine_w, got_w], 2), "section", axis=1, tiled=True, axis_index_groups=Z_GROUPS
    )
    got_bwd = to_row(bwd)
    fwd_y = (to_y(fwd, 1), to_y(fwd, -1), to_y(fwd, 2))
    right_own, right_other = own_units(pair, row, up_right[0].T)
    left_own, left_other = own_units(pair, row, down_left[0])
    got_bwd, right_other, left_other, *fwd_y = together(got_bwd, right_other, left_other, *fwd_y)
    bwd = all_channels(bwd, got_bwd)
    pair_bwd = to_pair(bwd)
    got_units = to_pair(jnp.stack([right_other, left_other]))
    fwd = jnp.stack([fwd, *fwd_y])
    got_fwd = to_row(fwd)
    bwd = jnp.stack([bwd, pair_bwd])
    bwd_y = (to_y(bwd, 1), to_y(bwd, -1), to_y(bwd, 2))
    got_fwd, got_units, bwd = together(got_fwd, got_units, bwd)
    fwd = all_channels(fwd, got_fwd)
    pair_fwd = to_pair(fwd)
    bwd = jnp.stack([bwd, *bwd_y], 1).reshape(2, 4, 2, 32, 2816)
    core_bwd = to_core(bwd)
    in_right = jnp.stack([right_own, got_units[0]])
    out_left = jnp.stack([left_own, got_units[1]])
    bwd = jnp.transpose(jnp.stack([bwd, core_bwd], 1), (3, 0, 1, 2, 4, 5)).reshape(2, 2, 256, 2816)
    weights, bwd = together(weights, bwd)
    up, down = weights[0], weights[1]
    x_bwd, din_bwd = bwd[0, :, :, :2560], bwd[0, :, :, 2560:]
    cots, gdout = bwd[1, :, :, :2560], bwd[1, :, :, 2560:]

    pre_bwd = mm("fd,std->fst", up, x_bwd) + mm("sfr,str->fst", in_right, din_bwd)
    sigma = jax.nn.sigmoid(pre_bwd)
    hid_bwd = (pre_bwd * sigma).astype(BF16)
    slope = sigma * (1.0 + pre_bwd * (1.0 - sigma))
    hid_bwd, pair_fwd = together(hid_bwd, pair_fwd)
    fwd = jnp.stack([fwd, pair_fwd])
    grad_hid = mm("fd,std->fst", down, cots) + mm("sfr,str->fst", out_left, gdout)
    grad_pre = (grad_hid * slope).astype(BF16)
    units = jnp.stack([grad_pre, hid_bwd])
    grads = mm("ufst,ustd->ufd", units, bwd[:, :, :, :2560]).astype(BF16)
    total = lax.psum_scatter(
        grads, "section", scatter_dimension=1, tiled=True, axis_index_groups=Z_GROUPS
    )
    grads, units, grad_pre, hid_bwd, fwd = together(grads, units, grad_pre, hid_bwd, fwd)
    low = jnp.concatenate(
        [mm("fst,sfr->str", hid_bwd, out_left), mm("fst,sfr->str", grad_pre, in_right)], 2
    )
    low = low.astype(BF16).reshape(2, 2, 4, 32, 512)
    core_low = to_core(low[:, 1])
    send_n = mm("fst,fd->std", grad_pre, up).astype(BF16).reshape(2, 2, 4, 32, 2560)
    core_n = to_core(send_n[:, 1])
    core_n, core_low, fwd, units = together(core_n, core_low, fwd, units)
    core_fwd = to_core(fwd)
    sum_n = jnp.concatenate(
        [add(send_n[:, 0], core_n).astype(BF16), add(low[:, 0], core_low).astype(BF16)], 3
    )
    total_n, sent_n = scatter_y(jnp.moveaxis(sum_n, 1, 0))
    pair_units = to_pair(units[:, :, 1])
    x_fwd = jnp.stack([fwd, core_fwd], 1).reshape(2, 256, 2816)
    x_fwd, din_fwd = x_fwd[:, :, :2560], x_fwd[:, :, 2560:]
    pre_fwd = mm("fd,std->fst", up, x_fwd) + mm("sfr,str->fst", in_right, din_fwd)
    hid_fwd = jax.nn.silu(pre_fwd).astype(BF16)
    hid_fwd, pair_units, *sent_n = together(hid_fwd, pair_units, *sent_n)
    sum_n = total_n(*sent_n)
    pair_n = to_pair(sum_n[1])
    half_units = jnp.stack([units[:, :, 0], pair_units], 1)
    other_units = to_row(half_units)
    send_f = jnp.concatenate(
        [mm("fst,fd->std", hid_fwd, down), mm("fst,sfr->str", hid_fwd, out_left)], 2
    )
    send_f = send_f.astype(BF16).reshape(2, 2, 4, 32, 2816)
    core_f = to_core(send_f[:, 1])
    send_f, core_f, pair_n = together(send_f, core_f, pair_n)

    total_f, sent_f = scatter_y(jnp.moveaxis(add(send_f[:, 0], core_f).astype(BF16), 1, 0))
    sum_n = add(sum_n[0], pair_n).astype(BF16)
    row_n = to_row(sum_n[:, 1280:])
    row_n, other_units, total, *sent_f = together(row_n, other_units, total, *sent_f)

    sum_f = total_f(*sent_f)
    pair_f = to_pair(sum_f[1])
    got = to_row(total[:, :, 1280:])
    rest = add(sum_n[:, 2560:], row_n[:, 1280:]).astype(BF16)
    grad_in = add(cot, sum_n[:, :1280], row_n[:, :1280]) + mm("tr,dr->td", rest[:, 256:], in_left)
    grad_in = grad_in.astype(BF16)
    rest = (rest, to_y(rest, 1), to_y(rest, -1), to_y(rest, 2))
    hid_all = in_order(pair, row, half_units[1], other_units[1])
    pre_all = in_order(pair, row, half_units[0], other_units[0])
    grad_down_left = mm("ft,tr->fr", hid_all, gdout[0])
    grad_up_right = mm("tr,ft->rf", din_bwd[0], pre_all)
    pair_f, got, grad_in, grad_down_left, grad_up_right, *rest = together(
        pair_f, got, grad_in, grad_down_left, grad_up_right, *rest
    )

    sum_f = add(sum_f[0], pair_f).astype(BF16)
    row_f = to_row(sum_f[:, 1280:])
    rest = jnp.stack(rest)
    rest = jnp.concatenate([rest, to_core(rest)], 0).reshape(256, 512)
    grad_down_right = mm("tr,td->rd", rest[:, :256], bwd[1, 0, :, :1280])
    grad_up_left = mm("td,tr->dr", bwd[0, 0, :, :1280], rest[:, 256:])
    row_f, grad_in, grad_down_right, grad_up_left = together(row_f, grad_in, grad_down_right, grad_up_left)
    handoff_bwd = to_section(grad_in, -1)
    dout_own = add(sum_f[:, 2560:], row_f[:, 1280:]).astype(BF16)
    out_fwd = add(in_fwd, sum_f[:, :1280], row_f[:, :1280]) + mm("tr,rd->td", dout_own, out_right)
    handoff_fwd = to_section(out_fwd.astype(BF16), 1)
    return (
        handoff_fwd[None],
        handoff_bwd[None],
        from_row(row, total[0, :, :1280], got[0]).T,
        from_row(row, total[1, :, :1280], got[1]),
        grad_up_left[None],
        grad_up_right[None],
        grad_down_left[None],
        grad_down_right[None],
    )


def solution(mesh):
    in_specs = (
        P("section", "col", "row"),
        P("section", "col", "row"),
        P("section", "col", "row"),
        P("row", ("col", "section")),
        P(("col", "section"), "row"),
        P("section", "row", None),
        P("section", None, "col"),
        P("section", "col", None),
        P("section", None, "row"),
    )
    out_specs = (
        P("section", "col", "row"),
        P("section", "col", "row"),
        P("row", ("col", "section")),
        P(("col", "section"), "row"),
        P("section", "row", None),
        P("section", None, "col"),
        P("section", "col", None),
        P("section", None, "row"),
    )
    return jax.shard_map(local, mesh=mesh, in_specs=in_specs, out_specs=out_specs, check_vma=False)
```

```python
import jax
import jax.numpy as jnp
import numpy as np
from jax import lax
from jax.sharding import PartitionSpec as P

F32 = jnp.float32
BF16 = jnp.bfloat16
PLACE = (2, 8, 2, 4, 2)
AXES = ("section", "row", "col")
Z_GROUPS = [list(range(8)), list(range(8, 16))]


def send(block, move):
    route = []
    for src in np.ndindex(*PLACE):
        dst = tuple(int(d) % n for d, n in zip(move(*src), PLACE))
        route.append((int(np.ravel_multi_index(src, PLACE)), int(np.ravel_multi_index(dst, PLACE))))
    return lax.ppermute(block, AXES, route)


def to_pair(block):
    return send(block, lambda a, z, r, y, k: (a + 1, z, r, y, k))


def to_row(block):
    return send(block, lambda a, z, r, y, k: (a, z, r + 1, y, k))


def to_core(block):
    return send(block, lambda a, z, r, y, k: (a, z, r, y, k + 1))


def to_y(block, hop):
    return send(block, lambda a, z, r, y, k: (a, z, r, y + hop, k))


def to_section(block, hop):
    def move(a, z, r, y, k):
        s = (a * 8 + z + hop) % 16
        return (s // 8, s % 8, r, y, k)

    return send(block, move)


def pick(block, index, axis):
    return lax.dynamic_index_in_dim(block, index, axis, keepdims=False)


def mm(subscripts, left, right):
    return jnp.einsum(subscripts, left, right, preferred_element_type=F32)


def add(*terms):
    total = terms[0].astype(F32)
    for term in terms[1:]:
        total = total + term.astype(F32)
    return total


def together(*blocks):
    return lax.optimization_barrier(blocks)


def tokens_first(block, part):
    return jnp.concatenate([block, part], -1)


def all_channels(mine, other):
    return jnp.concatenate(
        [mine[..., :1280], other[..., :1280], add(mine[..., 1280:], other[..., 1280:]).astype(BF16)], -1
    )


def scatter_y(block):
    sent = (to_y(block[1], -1), to_y(block[2], 1), to_y(block[3], 2))
    return lambda *got: add(block[0], *got).astype(BF16), sent


def from_row(row, mine, other):
    first = jnp.where(row == 0, mine, other)
    second = jnp.where(row == 0, other, mine)
    return jnp.concatenate([first, second], 0)


def in_order(pair, row, half, other):
    whole = jnp.stack([half, other]).reshape(2, 2, 8, 64, 256)
    whole = jnp.where(row == 0, whole, whole[::-1])
    whole = jnp.where(pair == 0, whole, whole[:, ::-1])
    return jnp.transpose(whole, (1, 2, 0, 3, 4)).reshape(2048, 256)


def own_units(pair, row, factor):
    units = pick(factor.reshape(2, 8, 2, 64, 256), row, 2)
    mine, other = pick(units, pair, 0), pick(units, 1 - pair, 0)
    return mine.reshape(512, 256), other.reshape(512, 256)


def local(
    input_fwd,
    input_bwd,
    cotangent,
    shared_up,
    shared_down,
    up_left,
    up_right,
    down_left,
    down_right,
):
    section, row = lax.axis_index("section"), lax.axis_index("row")
    pair = section // 8
    in_fwd, in_bwd, cot = input_fwd[0], input_bwd[0], cotangent[0]
    in_left, out_right = up_left[0], down_right[0]

    halves = jnp.stack([shared_up.T, shared_down]).reshape(2, 2, 64, 1280)
    mine_w = pick(halves, row, 1)
    give_w = pick(halves, 1 - row, 1)
    got_w = to_row(give_w)
    give_w, in_fwd, in_bwd, cot = together(give_w, in_fwd, in_bwd, cot)

    fwd = tokens_first(in_fwd, mm("td,dr->tr", in_fwd, in_left).astype(BF16))
    bwd = jnp.concatenate(
        [
            tokens_first(in_bwd, mm("td,dr->tr", in_bwd, in_left).astype(BF16)),
            tokens_first(cot, mm("td,rd->tr", cot, out_right).astype(BF16)),
        ],
        0,
    )
    got_w, bwd, fwd = together(got_w, bwd, fwd)

    weights = lax.all_gather(
        jnp.concatenate([mine_w, got_w], 2), "section", axis=1, tiled=True, axis_index_groups=Z_GROUPS
    )
    got_bwd = to_row(bwd)
    fwd_y = (to_y(fwd, 1), to_y(fwd, -1), to_y(fwd, 2))
    right_own, right_other = own_units(pair, row, up_right[0].T)
    left_own, left_other = own_units(pair, row, down_left[0])
    got_bwd, right_other, left_other, *fwd_y = together(got_bwd, right_other, left_other, *fwd_y)
    bwd = all_channels(bwd, got_bwd)
    pair_bwd = to_pair(bwd)
    got_units = to_pair(jnp.stack([right_other, left_other]))
    fwd = jnp.stack([fwd, *fwd_y])
    got_fwd = to_row(fwd)
    bwd = jnp.stack([bwd, pair_bwd])
    bwd_y = (to_y(bwd, 1), to_y(bwd, -1), to_y(bwd, 2))
    got_fwd, got_units, bwd = together(got_fwd, got_units, bwd)
    fwd = all_channels(fwd, got_fwd)
    pair_fwd = to_pair(fwd)
    bwd = jnp.stack([bwd, *bwd_y], 1).reshape(2, 4, 2, 32, 2816)
    core_bwd = to_core(bwd)
    in_right = jnp.stack([right_own, got_units[0]])
    out_left = jnp.stack([left_own, got_units[1]])
    bwd = jnp.transpose(jnp.stack([bwd, core_bwd], 1), (3, 0, 1, 2, 4, 5)).reshape(2, 2, 256, 2816)
    weights, bwd = together(weights, bwd)
    up, down = weights[0], weights[1]
    x_bwd, din_bwd = bwd[0, :, :, :2560], bwd[0, :, :, 2560:]
    cots, gdout = bwd[1, :, :, :2560], bwd[1, :, :, 2560:]

    pre_bwd = mm("fd,std->fst", up, x_bwd) + mm("sfr,str->fst", in_right, din_bwd)
    sigma = jax.nn.sigmoid(pre_bwd)
    hid_bwd = (pre_bwd * sigma).astype(BF16)
    slope = sigma * (1.0 + pre_bwd * (1.0 - sigma))
    hid_bwd, pair_fwd = together(hid_bwd, pair_fwd)
    fwd = jnp.stack([fwd, pair_fwd])
    grad_hid = mm("fd,std->fst", down, cots) + mm("sfr,str->fst", out_left, gdout)
    grad_pre = (grad_hid * slope).astype(BF16)
    units = jnp.stack([grad_pre, hid_bwd])
    grads = mm("ufst,ustd->ufd", units, bwd[:, :, :, :2560]).astype(BF16)
    total = lax.psum_scatter(
        grads, "section", scatter_dimension=1, tiled=True, axis_index_groups=Z_GROUPS
    )
    grads, units, grad_pre, hid_bwd, fwd = together(grads, units, grad_pre, hid_bwd, fwd)
    low = jnp.concatenate(
        [mm("fst,sfr->str", hid_bwd, out_left), mm("fst,sfr->str", grad_pre, in_right)], 2
    )
    low = low.astype(BF16).reshape(2, 2, 4, 32, 512)
    core_low = to_core(low[:, 1])
    send_n = mm("fst,fd->std", grad_pre, up).astype(BF16).reshape(2, 2, 4, 32, 2560)
    core_n = to_core(send_n[:, 1])
    core_n, core_low, fwd, units = together(core_n, core_low, fwd, units)
    core_fwd = to_core(fwd)
    sum_n = jnp.concatenate(
        [add(send_n[:, 0], core_n).astype(BF16), add(low[:, 0], core_low).astype(BF16)], 3
    )
    total_n, sent_n = scatter_y(jnp.moveaxis(sum_n, 1, 0))
    pair_units = to_pair(units[:, :, 1])
    x_fwd = jnp.stack([fwd, core_fwd], 1).reshape(2, 256, 2816)
    x_fwd, din_fwd = x_fwd[:, :, :2560], x_fwd[:, :, 2560:]
    pre_fwd = mm("fd,std->fst", up, x_fwd) + mm("sfr,str->fst", in_right, din_fwd)
    hid_fwd = jax.nn.silu(pre_fwd).astype(BF16)
    hid_fwd, pair_units = together(hid_fwd, pair_units)
    half_units = jnp.stack([units[:, :, 0], pair_units], 1)
    hid_fwd, half_units, *sent_n = together(hid_fwd, half_units, *sent_n)
    other_units = to_row(half_units)
    sum_n = total_n(*sent_n)
    pair_n = to_pair(sum_n[1])
    send_f = jnp.concatenate(
        [mm("fst,fd->std", hid_fwd, down), mm("fst,sfr->str", hid_fwd, out_left)], 2
    )
    send_f = send_f.astype(BF16).reshape(2, 2, 4, 32, 2816)
    core_f = to_core(send_f[:, 1])
    send_f, core_f, pair_n = together(send_f, core_f, pair_n)

    total_f, sent_f = scatter_y(jnp.moveaxis(add(send_f[:, 0], core_f).astype(BF16), 1, 0))
    sum_n = add(sum_n[0], pair_n).astype(BF16)
    row_n = to_row(sum_n[:, 1280:])
    row_n, other_units, total, *sent_f = together(row_n, other_units, total, *sent_f)

    sum_f = total_f(*sent_f)
    pair_f = to_pair(sum_f[1])
    got = to_row(total[:, :, 1280:])
    rest = add(sum_n[:, 2560:], row_n[:, 1280:]).astype(BF16)
    grad_in = add(cot, sum_n[:, :1280], row_n[:, :1280]) + mm("tr,dr->td", rest[:, 256:], in_left)
    grad_in = grad_in.astype(BF16)
    rest = (rest, to_y(rest, 1), to_y(rest, -1), to_y(rest, 2))
    hid_all = in_order(pair, row, half_units[1], other_units[1])
    pre_all = in_order(pair, row, half_units[0], other_units[0])
    grad_down_left = mm("ft,tr->fr", hid_all, gdout[0])
    grad_up_right = mm("tr,ft->rf", din_bwd[0], pre_all)
    pair_f, got, grad_in, grad_down_left, grad_up_right, *rest = together(
        pair_f, got, grad_in, grad_down_left, grad_up_right, *rest
    )

    sum_f = add(sum_f[0], pair_f).astype(BF16)
    row_f = to_row(sum_f[:, 1280:])
    rest = jnp.stack(rest)
    rest = jnp.concatenate([rest, to_core(rest)], 0).reshape(256, 512)
    grad_down_right = mm("tr,td->rd", rest[:, :256], bwd[1, 0, :, :1280])
    grad_up_left = mm("td,tr->dr", bwd[0, 0, :, :1280], rest[:, 256:])
    row_f, grad_in, grad_down_right, grad_up_left = together(row_f, grad_in, grad_down_right, grad_up_left)
    handoff_bwd = to_section(grad_in, -1)
    dout_own = add(sum_f[:, 2560:], row_f[:, 1280:]).astype(BF16)
    out_fwd = add(in_fwd, sum_f[:, :1280], row_f[:, :1280]) + mm("tr,rd->td", dout_own, out_right)
    handoff_fwd = to_section(out_fwd.astype(BF16), 1)
    return (
        handoff_fwd[None],
        handoff_bwd[None],
        from_row(row, total[0, :, :1280], got[0]).T,
        from_row(row, total[1, :, :1280], got[1]),
        grad_up_left[None],
        grad_up_right[None],
        grad_down_left[None],
        grad_down_right[None],
    )


def solution(mesh):
    in_specs = (
        P("section", "col", "row"),
        P("section", "col", "row"),
        P("section", "col", "row"),
        P("row", ("col", "section")),
        P(("col", "section"), "row"),
        P("section", "row", None),
        P("section", None, "col"),
        P("section", "col", None),
        P("section", None, "row"),
    )
    out_specs = (
        P("section", "col", "row"),
        P("section", "col", "row"),
        P("row", ("col", "section")),
        P(("col", "section"), "row"),
        P("section", "row", None),
        P("section", None, "col"),
        P("section", "col", None),
        P("section", None, "row"),
    )
    return jax.shard_map(local, mesh=mesh, in_specs=in_specs, out_specs=out_specs, check_vma=False)
```
